32 devices in a mesh: dp: 2 (over y), blk: 4 (over z), tensor: 4 (over x, core).
Axes of the slice: x: 2, y: 2, z: 4, core: 2. Of those that a mesh axis runs over, the one named last changes fastest.
Arguments:
- target: bfloat16 [16, 512, 1024], P('dp', 'blk'), may hold values from -6 to 6
- source: bfloat16 [16, 4096, 1024], P('dp', 'blk'), may hold values from -6 to 6
- target_segments: int32 [16, 512], P('dp', 'blk'), may hold values from 0 to 15, never falling along the last dimension, each value on 1 to 80 neighbouring positions
- source_segments: int32 [16, 4096], P('dp', 'blk'), may hold values from 0 to 15, never falling along the last dimension, each value on 1 to 1024 neighbouring positions
- self_query: bfloat16 [1024, 1024], P(None, 'tensor'), may hold values from -0.1875 to 0.1875
- self_key: bfloat16 [1024, 1024], P(None, 'tensor'), may hold values from -0.1875 to 0.1875
- self_value: bfloat16 [1024, 1024], P(None, 'tensor'), may hold values from -0.1875 to 0.1875
- self_output: bfloat16 [1024, 1024], P('tensor'), may hold values from -0.75 to 0.75
- cross_query: bfloat16 [1024, 1024], P(None, 'tensor'), may hold values from -0.1875 to 0.1875
- cross_key: bfloat16 [1024, 1024], P(None, 'tensor'), may hold values from -0.1875 to 0.1875
- cross_value: bfloat16 [1024, 1024], P(None, 'tensor'), may hold values from -0.1875 to 0.1875
- cross_output: bfloat16 [1024, 1024], P('tensor'), may hold values from -1 to 1
- ffn_in: bfloat16 [1024, 4096], P(None, 'tensor'), may hold values from -0.1875 to 0.1875
- ffn_out: bfloat16 [4096, 1024], P('tensor'), may hold values from -0.09375 to 0.09375
- adapter_down: bfloat16 [1024, 512], P(None, 'tensor'), may hold values from -0.1875 to 0.1875
- adapter_up: bfloat16 [512, 1024], P('tensor'), may hold values from -0.0625 to 0.0625
- first_gain: float32 [1024], replicated, may hold values from 0.5 to 1.5
- first_shift: float32 [1024], replicated, may hold values from -3 to 3
- second_gain: float32 [1024], replicated, may hold values from 0.5 to 1.5
- second_shift: float32 [1024], replicated, may hold values from -3 to 3
- third_gain: float32 [1024], replicated, may hold values from 0.5 to 1.5
- third_shift: float32 [1024], replicated, may hold values from -3 to 3
- out_cotangent: bfloat16 [16, 512, 1024], P('dp', 'blk'), may hold values from -6 to 6
Outputs:
- output: bfloat16 [16, 512, 1024], P('dp', 'blk')
- target_grad: float32 [16, 512, 1024], P('dp', 'blk')
- source_grad: float32 [16, 4096, 1024], P('dp', 'blk', 'tensor')
- self_query_grad: float32 [1024, 1024], P(None, 'tensor')
- self_key_grad: float32 [1024, 1024], P(None, 'tensor')
- self_value_grad: float32 [1024, 1024], P(None, 'tensor')
- self_output_grad: float32 [1024, 1024], P('tensor')
- cross_query_grad: float32 [1024, 1024], P(None, 'tensor')
- cross_key_grad: float32 [1024, 1024], P(None, 'tensor')
- cross_value_grad: float32 [1024, 1024], P(None, 'tensor')
- cross_output_grad: float32 [1024, 1024], P('tensor')
- adapter_down_grad: float32 [1024, 512], P(None, 'tensor')
- adapter_up_grad: float32 [512, 1024], P('tensor')
- first_gain_grad: float32 [1024], P('tensor')
- first_shift_grad: float32 [1024], P('tensor')
- second_gain_grad: float32 [1024], P('tensor')
- second_shift_grad: float32 [1024], P('tensor')
- third_gain_grad: float32 [1024], P('tensor')
- third_shift_grad: float32 [1024], P('tensor')
The draws below stay inside these ranges and needn't reach their ends.
Inputs may be any that keep to these rules, and one draw needn't show every extreme that they name: `target_segments`: in every row both id sequences never fall and hold each id 0 to 15; a summary has 1 to 80 slots and some has exactly 80; a document has 1 to 1024 slots and some has exactly 1024. `source_segments`: document ids pair with summary ids of the same row.
All inputs are finite; a program needn't handle non-finite values.
Results may differ from the reference program's by a relative error of at most 0.022.
Values may be sent and summed in bfloat16 or wider, within the bound.
No kernel may reach another device: no remote copies, remote signals or barrier semaphores. Data moves between devices by JAX's collectives and lax.ppermute only.
A program may use at most 320 MiB of HBM per device.

```python
import math
import jax
import jax.numpy as jnp
import numpy as np
from jax import lax

D = 1024
HEADS = 16
HEAD_DIM = 64
FF = 4096
ADAPTER = 512
SEGS = 16
MOST_T = 80
MOST_S = 1024
ROWS = 16
TLEN = 512
SLEN = 4096


def shard_levels(own_key, extent, split, least, top_value):
    level, own = 1.0, jax.random.fold_in(own_key, 6)
    for axis_at, blocks in split:
        steps = jnp.exp(jax.random.uniform(jax.random.fold_in(own, axis_at), (blocks,), jnp.float32, least / len(split), top_value / len(split)))
        level = level * jnp.repeat(steps, extent[axis_at] // blocks).reshape([-1 if axis == axis_at else 1 for axis in range(len(extent))])
    return level


def profile(number_of, total, bound, slope):
    loads = [(1 << 20) // math.isqrt(grade ** slope) + 1 for grade in range(2, number_of + 1)]
    spare, holding = total - bound - (number_of - 1), [1] * (number_of - 1)
    while spare > 0:
        free = [i for i in range(number_of - 1) if holding[i] < bound]
        pool, budget = sum([loads[i] for i in free]), spare
        for i in free:
            extra = min(bound - holding[i], max(1, budget * loads[i] // pool), spare)
            holding[i] = holding[i] + extra
            spare = spare - extra
    return np.array([bound] + holding)


def uneven(rng, amount, total, bound, slope):
    if amount == 2:
        one = jax.random.randint(rng, (), max(1, total - bound), min(bound, total - 1) + 1)
        return jnp.stack([one, total - one])
    tallies = jnp.asarray(profile(amount, total, bound, slope), jnp.int32)
    pairs = (amount - 1) // 2
    giver, sink = tallies[1:1 + 2 * pairs:2], tallies[2:2 + 2 * pairs:2]
    slack = jnp.minimum(giver - 1, bound - sink)
    passed = jax.random.randint(jax.random.fold_in(rng, 1), (pairs,), 0, 1 << 20) % (slack + 1)
    tallies = tallies.at[1:1 + 2 * pairs:2].set(giver - passed).at[2:2 + 2 * pairs:2].set(sink + passed)
    return tallies[jax.random.permutation(jax.random.fold_in(rng, 2), amount)]


def bell_draw(key, shape, width, bound, split=(), dtype=jnp.bfloat16):
    loudness = shard_levels(key, shape, split, -0.22, 0.18) if split else 1.0
    entries = jax.random.normal(key, shape, jnp.float32) * width * loudness
    return jnp.minimum(jnp.maximum(entries, -bound), bound).astype(dtype)


def setup_inputs(seed: int = 0) -> dict:
    arg_keys = jax.random.split(jax.random.key(seed), 24)
    target = bell_draw(arg_keys[0], (ROWS, TLEN, D), 1.0, 6.0, ((0, 2), (1, 4)))
    source = bell_draw(arg_keys[1], (ROWS, SLEN, D), 1.0, 6.0, ((0, 2), (1, 4)))
    target_segments = jax.vmap(lambda own: jnp.searchsorted(jnp.cumsum(uneven(own, SEGS, TLEN, MOST_T, 2)), jnp.arange(TLEN), side="right"))(jax.random.split(arg_keys[2], ROWS)).reshape((ROWS, TLEN)).astype(jnp.int32)
    source_segments = jax.vmap(lambda own: jnp.searchsorted(jnp.cumsum(uneven(own, SEGS, SLEN, MOST_S, 2)), jnp.arange(SLEN), side="right"))(jax.random.split(arg_keys[3], ROWS)).reshape((ROWS, SLEN)).astype(jnp.int32)
    self_query = bell_draw(arg_keys[4], (D, D), D ** -0.5, 0.1875, ((1, 4),))
    self_key = bell_draw(arg_keys[5], (D, D), D ** -0.5, 0.1875, ((1, 4),))
    self_value = bell_draw(arg_keys[6], (D, D), D ** -0.5, 0.1875, ((1, 4),))
    self_output = bell_draw(arg_keys[7], (D, D), (D // 16) ** -0.5, 0.75, ((0, 4),))
    cross_query = bell_draw(arg_keys[8], (D, D), D ** -0.5, 0.1875, ((1, 4),))
    cross_key = bell_draw(arg_keys[9], (D, D), D ** -0.5, 0.1875, ((1, 4),))
    cross_value = bell_draw(arg_keys[10], (D, D), D ** -0.5, 0.1875, ((1, 4),))
    cross_output = bell_draw(arg_keys[11], (D, D), (D // 32) ** -0.5, 1.0, ((0, 4),))
    ffn_in = bell_draw(arg_keys[12], (D, FF), D ** -0.5, 0.1875, ((1, 4),))
    ffn_out = bell_draw(arg_keys[13], (FF, D), FF ** -0.5, 0.09375, ((0, 4),))
    adapter_down = bell_draw(arg_keys[14], (D, ADAPTER), D ** -0.5, 0.1875, ((1, 4),))
    adapter_up = bell_draw(arg_keys[15], (ADAPTER, D), (16 * ADAPTER) ** -0.5, 0.0625, ((0, 4),))
    first_gain = jnp.clip(1.0 + 0.1 * jax.random.normal(arg_keys[16], (D,), jnp.float32), 0.5, 1.5)
    first_shift = bell_draw(arg_keys[17], (D,), 0.5, 3.0, (), jnp.float32)
    second_gain = jnp.clip(1.0 + 0.1 * jax.random.normal(arg_keys[18], (D,), jnp.float32), 0.5, 1.5)
    second_shift = bell_draw(arg_keys[19], (D,), 0.5, 3.0, (), jnp.float32)
    third_gain = jnp.clip(1.0 + 0.1 * jax.random.normal(arg_keys[20], (D,), jnp.float32), 0.5, 1.5)
    third_shift = bell_draw(arg_keys[21], (D,), 0.5, 3.0, (), jnp.float32)
    out_cotangent = bell_draw(arg_keys[22], (ROWS, TLEN, D), 1.0, 6.0, ((0, 2), (1, 4)))
    return {"target": target, "source": source, "target_segments": target_segments, "source_segments": source_segments, "self_query": self_query, "self_key": self_key, "self_value": self_value, "self_output": self_output, "cross_query": cross_query, "cross_key": cross_key, "cross_value": cross_value, "cross_output": cross_output, "ffn_in": ffn_in, "ffn_out": ffn_out, "adapter_down": adapter_down, "adapter_up": adapter_up, "first_gain": first_gain, "first_shift": first_shift, "second_gain": second_gain, "second_shift": second_shift, "third_gain": third_gain, "third_shift": third_shift, "out_cotangent": out_cotangent}


precise = lax.Precision.HIGHEST
epsilon = 1e-05

@jax.custom_vjp
def low(v):
    return lax.optimization_barrier(v.astype(jnp.bfloat16)).astype(jnp.float32)

@jax.custom_vjp
def low_back(v):
    return v

def low_keep(v):
    return (low(v), None)

def low_pass(kept, grad):
    return (grad,)

def back_keep(v):
    return (v, None)

def back_low(kept, grad):
    return (low(grad),)
low.defvjp(low_keep, low_pass)
low_back.defvjp(back_keep, back_low)

def matmul(left, right):
    return jnp.matmul(left, right, precision=precise)

def layer_norm(values, gain, shift):
    centered = values - lax.optimization_barrier(jnp.mean(values, axis=-1, keepdims=True))
    variance = lax.optimization_barrier(jnp.mean(centered * centered, axis=-1, keepdims=True))
    return centered * lax.rsqrt(variance + epsilon) * gain + shift

def attend(queries, keys, values, allowed):
    length_query = queries.shape[0]
    length_key = keys.shape[0]
    queries = queries.reshape(length_query, HEADS, HEAD_DIM)
    keys = keys.reshape(length_key, HEADS, HEAD_DIM)
    values = values.reshape(length_key, HEADS, HEAD_DIM)
    scores = low_back(jnp.einsum('qhd,khd->hqk', queries, keys, precision=precise) * HEAD_DIM ** (-0.5))
    masked = jnp.where(allowed[None], scores, -1e+30)
    highest = lax.optimization_barrier(jnp.max(masked, axis=-1, keepdims=True))
    weights = jnp.where(allowed[None], jnp.exp(masked - highest), 0.0)
    totals = lax.optimization_barrier(jnp.sum(weights, axis=-1))
    mixed = jnp.einsum('hqk,khd->qhd', weights, values, precision=precise)
    mixed = mixed / jnp.transpose(totals)[:, :, None]
    return mixed.reshape(length_query, HEADS * HEAD_DIM)

def row_layer(params, frozen, row):
    self_query, self_key, self_value, self_output, cross_query, cross_key, cross_value, cross_output, adapter_down, adapter_up, first_gain, first_shift, second_gain, second_shift, third_gain, third_shift = params
    ffn_in, ffn_out = frozen
    target, source, target_ids, source_ids = row
    places = jnp.arange(target.shape[0])
    causal = (target_ids[:, None] == target_ids[None, :]) & (places[None, :] <= places[:, None])
    crossing = target_ids[:, None] == source_ids[None, :]
    queries = low(low_back(matmul(target, self_query)))
    keys = low(low_back(matmul(target, self_key)))
    values = low(low_back(matmul(target, self_value)))
    mixed = low(low_back(attend(queries, keys, values, causal)))
    first = layer_norm(target + low_back(matmul(mixed, self_output)), first_gain, first_shift)
    first_low = low(first)
    cross_queries = low(low_back(matmul(first_low, cross_query)))
    cross_keys = low(low_back(matmul(source, cross_key)))
    cross_values = low(low_back(matmul(source, cross_value)))
    cross_mixed = low(low_back(attend(cross_queries, cross_keys, cross_values, crossing)))
    second = layer_norm(first + low_back(matmul(cross_mixed, cross_output)), second_gain, second_shift)
    second_low = low(second)
    gate = low_back(matmul(second_low, ffn_in))
    active = low(jax.nn.gelu(gate, approximate=False))
    down = low_back(matmul(second_low, adapter_down))
    rectified = low(jax.nn.silu(down))
    branch = low_back(matmul(active, ffn_out) + 4.0 * matmul(rectified, adapter_up))
    return layer_norm(second + branch, third_gain, third_shift)

def reference(target, source, target_segments, source_segments, self_query, self_key, self_value, self_output, cross_query, cross_key, cross_value, cross_output, ffn_in, ffn_out, adapter_down, adapter_up, first_gain, first_shift, second_gain, second_shift, third_gain, third_shift, out_cotangent):
    params = tuple((p.astype(jnp.float32) for p in (self_query, self_key, self_value, self_output, cross_query, cross_key, cross_value, cross_output, adapter_down, adapter_up, first_gain, first_shift, second_gain, second_shift, third_gain, third_shift)))
    frozen = (ffn_in.astype(jnp.float32), ffn_out.astype(jnp.float32))

    def forward(target_full, source_full, weights):

        def one_row(row):
            return row_layer(weights, frozen, row)
        return lax.map(jax.checkpoint(one_row), (target_full, source_full, target_segments, source_segments))
    result, pullback = jax.vjp(forward, target.astype(jnp.float32), source.astype(jnp.float32), params)
    target_grad, source_grad, grads = pullback(out_cotangent.astype(jnp.float32))
    return (result.astype(jnp.bfloat16), target_grad, source_grad, grads[0], grads[1], grads[2], grads[3], grads[4], grads[5], grads[6], grads[7], grads[8], grads[9], grads[10], grads[11], grads[12], grads[13], grads[14], grads[15])
```

```python
import functools

import jax
import jax.numpy as jnp
from jax import lax
from jax.experimental import pallas as pl
from jax.experimental.pallas import tpu as pltpu
from jax.sharding import PartitionSpec as P

HEAD_DIM = 64
HALO = 80
CHUNKS = 1
SOURCE_TILE = 256

epsilon = 1e-05
negative = -1e30
floor = -1e20
log2e = 1.4426950408889634
to_base2 = log2e * HEAD_DIM**-0.5
bf16 = jnp.bfloat16
f32 = jnp.float32


def forward_mul(left, right):
    return jnp.einsum("rti,ij->rtj", left, right, preferred_element_type=f32)


def backward_mul(left, right):
    return jnp.einsum("rtj,ij->rti", left, right, preferred_element_type=f32)


def weight_mul(left, right):
    return jnp.einsum("rti,rtj->ij", left, right, preferred_element_type=f32)


def norm_parts(values):
    centered = values - jnp.mean(values, axis=-1, keepdims=True)
    variance = jnp.mean(centered * centered, axis=-1, keepdims=True)
    scale = lax.rsqrt(variance + epsilon)
    return centered * scale, scale


def norm_back(unit, scale, gain, grad):
    inner = grad * gain
    first = jnp.mean(inner, axis=-1, keepdims=True)
    second = jnp.mean(inner * unit, axis=-1, keepdims=True)
    return (
        scale * (inner - first - unit * second),
        jnp.sum(grad * unit, axis=(0, 1)),
        jnp.sum(grad, axis=(0, 1)),
    )


def mul_nt(left, right):
    return lax.dot_general(left, right, (((1,), (1,)), ((), ())), preferred_element_type=f32)


def mul_nn(left, right):
    return lax.dot_general(left, right, (((1,), (0,)), ((), ())), preferred_element_type=f32)


def spread_heads(block, heads):
    if heads == 1:
        return block
    width = block.shape[1]
    lane = lax.broadcasted_iota(jnp.int32, (1, width), 1)
    copies = []
    for head in range(heads):
        inside = (lane >= head * HEAD_DIM) & (lane < (head + 1) * HEAD_DIM)
        copies.append(block * jnp.where(inside, 1.0, 0.0).astype(block.dtype))
    return jnp.concatenate(copies, axis=0)


def tile_lanes(block, heads):
    return jnp.concatenate([block] * heads, axis=1) if heads > 1 else block


def row_of(ref, heads):
    rows = [ref[0, head : head + 1, :] for head in range(heads)]
    return jnp.concatenate(rows, axis=1) if heads > 1 else rows[0]


def store_rows(ref, row, heads, count):
    for head in range(heads):
        ref[0, head : head + 1, :] = row[:, head * count : (head + 1) * count]


def head_products(left, right, heads, count):
    pieces = [
        mul_nn(
            left[head * HEAD_DIM : (head + 1) * HEAD_DIM, :],
            right[:, head * count : (head + 1) * count],
        )
        for head in range(heads)
    ]
    return jnp.concatenate(pieces, axis=0) if heads > 1 else pieces[0]


def head_scale(row, heads, count):
    pieces = [
        jnp.broadcast_to(row[:, head * count : (head + 1) * count], (HEAD_DIM, count))
        for head in range(heads)
    ]
    return jnp.concatenate(pieces, axis=0) if heads > 1 else pieces[0]


def cross_forward_kernel(heads, blocks, tile, shift_ref, table_ref, *refs):
    queries = refs[:blocks]
    target_ids, source_ids, keys, values = refs[blocks : blocks + 4]
    mixed = refs[blocks + 4 : 2 * blocks + 4]
    sums = refs[2 * blocks + 4 : 3 * blocks + 4]
    turned, total = refs[3 * blocks + 4 :]
    place = pl.program_id(0)
    count = queries[0].shape[1]
    tiles = keys.shape[1] // tile
    for step in range(tiles):
        turned[step] = values[0, step * tile : (step + 1) * tile, :].T
    for block in range(blocks):
        spread = spread_heads(queries[block][0], heads)
        ids = target_ids[0, block : block + 1, :]
        total[...] = jnp.zeros_like(total)

        def visit(step, carry):
            best, weight = carry
            start = pl.multiple_of(step * tile, tile)
            scores = mul_nt(keys[0, pl.ds(start, tile), :], spread) * to_base2
            allowed = source_ids[0, pl.ds(start, tile), :] == ids
            scores = jnp.where(tile_lanes(allowed, heads), scores, negative)
            fresh = jnp.maximum(best, jnp.max(scores, axis=0, keepdims=True))
            anchor = jnp.maximum(fresh, floor)
            probs = jnp.exp2(scores - anchor)
            fade = jnp.exp2(best - anchor)
            weight = weight * fade + jnp.sum(probs, axis=0, keepdims=True)
            total[...] = total[...] * head_scale(fade, heads, count) + head_products(
                turned[step], probs.astype(bf16), heads, count
            )
            return fresh, weight

        best, weight = lax.fori_loop(
            table_ref[place, 2 * block],
            table_ref[place, 2 * block + 1],
            visit,
            (jnp.full((1, heads * count), negative, f32), jnp.zeros((1, heads * count), f32)),
        )
        some = weight > 0.0
        safe = jnp.where(some, weight, 1.0)
        scaled = total[...] * head_scale(1.0 / safe, heads, count)
        mixed[block][0] = scaled.T.astype(bf16)
        store_rows(sums[block], jnp.where(some, best + jnp.log2(safe), negative), heads, count)


def cross_backward_kernel(heads, blocks, tile, shift_ref, table_ref, *refs):
    queries = refs[:blocks]
    grads = refs[blocks : 2 * blocks]
    sums = refs[2 * blocks : 3 * blocks]
    deltas = refs[3 * blocks : 4 * blocks]
    target_ids, source_ids, keys, values = refs[4 * blocks : 4 * blocks + 4]
    query_grads = refs[4 * blocks + 4 : 5 * blocks + 4]
    source_side, turned, key_grad, value_grad, total = refs[5 * blocks + 4 :]
    place = pl.program_id(0)
    count = queries[0].shape[1]
    tiles = keys.shape[1] // tile
    for step in range(tiles):
        turned[step] = keys[0, step * tile : (step + 1) * tile, :].T
    key_grad[...] = jnp.zeros_like(key_grad)
    value_grad[...] = jnp.zeros_like(value_grad)
    for block in range(blocks):
        spread = spread_heads(queries[block][0], heads)
        spread_grad = spread_heads(grads[block][0], heads)
        offset = row_of(sums[block], heads)
        delta = row_of(deltas[block], heads)
        ids = target_ids[0, block : block + 1, :]
        total[...] = jnp.zeros_like(total)

        def visit(step, carry):
            start = pl.multiple_of(step * tile, tile)
            span = pl.ds(start, tile)
            scores = mul_nt(keys[0, span, :], spread) * to_base2
            allowed = source_ids[0, span, :] == ids
            probs = jnp.where(tile_lanes(allowed, heads), jnp.exp2(scores - offset), 0.0)
            dprobs = mul_nt(values[0, span, :], spread_grad)
            dscores = (probs * (dprobs - delta)).astype(bf16)
            key_grad[span, :] += mul_nn(dscores, spread)
            value_grad[span, :] += mul_nn(probs.astype(bf16), spread_grad)
            total[...] += head_products(turned[step], dscores, heads, count)
            return carry

        lax.fori_loop(table_ref[place, 2 * block], table_ref[place, 2 * block + 1], visit, 0)
        query_grads[block][0] = (total[...] * HEAD_DIM**-0.5).T.astype(bf16)
    source_side[0] = jnp.concatenate(
        [(key_grad[...] * HEAD_DIM**-0.5).astype(bf16), value_grad[...].astype(bf16)], axis=1
    )


def self_scores(heads, queries, keys, source_ids, ids):
    spread = spread_heads(queries, heads)
    scores = mul_nt(keys, spread) * to_base2
    count = queries.shape[0]
    slots = keys.shape[0]
    key_place = lax.broadcasted_iota(jnp.int32, (slots, count), 0) - (slots - count)
    query_place = lax.broadcasted_iota(jnp.int32, (slots, count), 1)
    allowed = (source_ids == ids) & (key_place <= query_place)
    return spread, scores, tile_lanes(allowed, heads)


def with_halo(halo, own):
    missing = own.shape[0] - halo.shape[0]
    return jnp.concatenate([jnp.zeros((missing, own.shape[1]), own.dtype), halo, own], axis=0)


def self_forward_kernel(heads, shift_ref, *refs):
    queries, keys, values, key_halo, value_halo, target_ids, source_ids, mixed, sums = refs
    count = queries.shape[1]
    every_key = with_halo(key_halo[0], keys[0])
    every_value = with_halo(value_halo[0], values[0])
    _, scores, allowed = self_scores(
        heads, queries[0], every_key, source_ids[0], target_ids[0, 0:1, :]
    )
    scores = jnp.where(allowed, scores, negative)
    best = jnp.max(scores, axis=0, keepdims=True)
    probs = jnp.exp2(scores - best)
    weight = jnp.sum(probs, axis=0, keepdims=True)
    total = head_products(every_value.T, probs.astype(bf16), heads, count)
    mixed[0] = (total * head_scale(1.0 / weight, heads, count)).T.astype(bf16)
    store_rows(sums, best + jnp.log2(weight), heads, count)


def self_backward_kernel(heads, shift_ref, *refs):
    queries, keys, values, key_halo, value_halo, target_ids, source_ids, sums, grads = refs[:9]
    query_grad, key_own, value_own, side = refs[9:]
    count = queries.shape[1]
    every_key = with_halo(key_halo[0], keys[0])
    every_value = with_halo(value_halo[0], values[0])
    spread, scores, allowed = self_scores(
        heads, queries[0], every_key, source_ids[0], target_ids[0, 0:1, :]
    )
    spread_grad = spread_heads(grads[0], heads)
    probs = jnp.where(allowed, jnp.exp2(scores - row_of(sums, heads)), 0.0)
    dprobs = mul_nt(every_value, spread_grad)
    delta = jnp.sum(probs * dprobs, axis=0, keepdims=True)
    dscores = (probs * (dprobs - delta)).astype(bf16)
    key_grad = mul_nn(dscores, spread) * HEAD_DIM**-0.5
    value_grad = mul_nn(probs.astype(bf16), spread_grad)
    total = head_products(every_key.T, dscores, heads, count)
    query_grad[0] = (total * HEAD_DIM**-0.5).T.astype(bf16)
    slots = every_key.shape[0]
    first = slots - count - HALO
    key_own[0] = key_grad[slots - count :, :]
    value_own[0] = value_grad[slots - count :, :]
    side[0] = jnp.concatenate(
        [
            key_grad[first : slots - count, :].astype(bf16),
            value_grad[first : slots - count, :].astype(bf16),
        ],
        axis=1,
    )


def column_block(array, index, width):
    if width % 128 == 0:
        return array, index
    return array[..., index * width : (index + 1) * width], 0


def rolled(rows, half):
    def at(step, shift):
        return lax.rem(step + shift[0] * half, rows)

    return at


def cross_call(backward, heads, queries, extra, target_ids, source_ids, kv, table, shift):
    blocks = len(queries)
    rows, count, width = queries[0].shape
    slots = kv.shape[1]
    tile = min(SOURCE_TILE, slots)
    keys, key_column = column_block(kv, 0, width)
    values, value_column = column_block(kv, 1, width)
    turn = rolled(rows, rows // 2)
    token = pl.BlockSpec((1, count, width), lambda i, s, t: (turn(i, s), 0, 0))
    stat = pl.BlockSpec((1, heads, count), lambda i, s, t: (turn(i, s), 0, 0))
    in_specs = [token] * blocks
    operands = list(queries)
    if backward:
        grads, sums, deltas = extra
        in_specs += [token] * blocks + [stat] * (2 * blocks)
        operands += list(grads) + list(sums) + list(deltas)
    in_specs += [
        pl.BlockSpec((1, blocks, count), lambda i, s, t: (i, 0, 0)),
        pl.BlockSpec((1, slots, 1), lambda i, s, t: (i, 0, 0)),
        pl.BlockSpec((1, slots, width), lambda i, s, t: (i, 0, key_column)),
        pl.BlockSpec((1, slots, width), lambda i, s, t: (i, 0, value_column)),
    ]
    operands += [target_ids, source_ids, keys, values]
    token_out = jax.ShapeDtypeStruct((rows, count, width), bf16)
    stat_out = jax.ShapeDtypeStruct((rows, heads, count), f32)
    scratch = [pltpu.VMEM((slots // tile, width, tile), bf16)]
    if backward:
        out_shape = [token_out] * blocks + [jax.ShapeDtypeStruct((rows, slots, 2 * width), bf16)]
        out_specs = [token] * blocks + [
            pl.BlockSpec((1, slots, 2 * width), lambda i, s, t: (i, 0, 0))
        ]
        scratch += [pltpu.VMEM((slots, width), f32), pltpu.VMEM((slots, width), f32)]
    else:
        out_shape = [token_out] * blocks + [stat_out] * blocks
        out_specs = [token] * blocks + [stat] * blocks
    scratch += [pltpu.VMEM((width, count), f32)]
    work = rows * slots * blocks * count * width // 2
    return pl.pallas_call(
        functools.partial(
            cross_backward_kernel if backward else cross_forward_kernel, heads, blocks, tile
        ),
        grid_spec=pltpu.PrefetchScalarGridSpec(
            num_scalar_prefetch=2,
            grid=(rows,),
            in_specs=in_specs,
            out_specs=out_specs,
            scratch_shapes=scratch,
        ),
        out_shape=out_shape,
        compiler_params=pltpu.CompilerParams(vmem_limit_bytes=40 * 2**20),
        cost_estimate=pl.CostEstimate(
            flops=work * (20 if backward else 8),
            bytes_accessed=rows * slots * width * (8 if backward else 4),
            transcendentals=0,
        ),
        name="cross_backward" if backward else "cross_forward",
    )(shift, table, *operands)


def self_call(backward, heads, qkv, halo, extra, target_ids, source_ids, width, shift):
    rows, count = qkv.shape[:2]
    turn = rolled(rows, rows // 2)
    in_specs, operands = [], []
    for index in range(3):
        operand, column = column_block(qkv, index, width)
        operands.append(operand)
        in_specs.append(
            pl.BlockSpec((1, count, width), lambda i, s, at=column: (turn(i, s), 0, at))
        )
    for index in range(2):
        operand, column = column_block(halo, index, width)
        operands.append(operand)
        in_specs.append(pl.BlockSpec((1, HALO, width), lambda i, s, at=column: (turn(i, s), 0, at)))
    token = pl.BlockSpec((1, count, width), lambda i, s: (turn(i, s), 0, 0))
    stat = pl.BlockSpec((1, heads, count), lambda i, s: (turn(i, s), 0, 0))
    in_specs += [
        pl.BlockSpec((1, 1, count), lambda i, s: (i, 0, 0)),
        pl.BlockSpec((1, 2 * count, 1), lambda i, s: (i, 0, 0)),
    ]
    operands += [target_ids, source_ids]
    token_shape = (rows, count, width)
    if backward:
        in_specs += [stat, token]
        operands += list(extra)
        out_shape = [
            jax.ShapeDtypeStruct(token_shape, bf16),
            jax.ShapeDtypeStruct(token_shape, f32),
            jax.ShapeDtypeStruct(token_shape, f32),
            jax.ShapeDtypeStruct((rows, HALO, 2 * width), bf16),
        ]
        out_specs = [
            token,
            token,
            token,
            pl.BlockSpec((1, HALO, 2 * width), lambda i, s: (turn(i, s), 0, 0)),
        ]
    else:
        out_shape = [
            jax.ShapeDtypeStruct(token_shape, bf16),
            jax.ShapeDtypeStruct((rows, heads, count), f32),
        ]
        out_specs = [token, stat]
    work = rows * count * count * width
    return pl.pallas_call(
        functools.partial(self_backward_kernel if backward else self_forward_kernel, heads),
        grid_spec=pltpu.PrefetchScalarGridSpec(
            num_scalar_prefetch=1, grid=(rows,), in_specs=in_specs, out_specs=out_specs
        ),
        out_shape=out_shape,
        compiler_params=pltpu.CompilerParams(vmem_limit_bytes=40 * 2**20),
        cost_estimate=pl.CostEstimate(
            flops=work * (40 if backward else 16),
            bytes_accessed=rows * count * width * 12,
            transcendentals=0,
        ),
        name="self_backward" if backward else "self_forward",
    )(shift, *operands)


def send_blk(array, distance, size):
    return lax.ppermute(array, "blk", [(i, (i + distance) % size) for i in range(size)])


def send_sibling(array, size):
    return lax.ppermute(array, "tensor", [(i, i ^ 1) for i in range(size)])


def settle(array):
    return lax.optimization_barrier(array.astype(bf16))


def sum_tensor(mine, other, size):
    total = mine + send_sibling(other.astype(bf16), size).astype(f32)
    step = 2
    while step < size:
        low = settle(total)
        total = low.astype(f32) + lax.ppermute(
            low, "tensor", [(i, i ^ step) for i in range(size)]
        ).astype(f32)
        step *= 2
    return total


def halves(array):
    half = array.shape[0] // 2
    return array[:half], array[half:]


def on_device(
    target,
    source,
    target_segments,
    source_segments,
    self_query,
    self_key,
    self_value,
    self_output,
    cross_query,
    cross_key,
    cross_value,
    cross_output,
    ffn_in,
    ffn_out,
    adapter_down,
    adapter_up,
    first_gain,
    first_shift,
    second_gain,
    second_shift,
    third_gain,
    third_shift,
    out_cotangent,
):
    rows, count, depth = target.shape
    slots = source.shape[1]
    width = self_query.shape[1]
    heads = width // HEAD_DIM
    blocks = lax.axis_size("blk")
    lanes = lax.axis_size("tensor")
    place = lax.axis_index("blk")
    core = lax.rem(lax.axis_index("tensor"), 2)
    shift = core.astype(jnp.int32).reshape(1)
    many = rows // CHUNKS
    half = many // 2
    tile = min(SOURCE_TILE, slots)

    far_ids = [target_segments] + [
        send_blk(target_segments, step, blocks) for step in range(1, blocks)
    ]
    target_ids = jnp.stack(far_ids, axis=1)
    tiles = source_segments.reshape(rows, slots // tile, tile)
    table = jnp.stack(
        [
            jnp.sum(tiles[:, None, :, -1] < target_ids[:, :, :1], axis=-1, dtype=jnp.int32),
            jnp.sum(tiles[:, None, :, 0] <= target_ids[:, :, -1:], axis=-1, dtype=jnp.int32),
        ],
        axis=-1,
    ).reshape(rows, 2 * blocks)
    source_ids = source_segments[:, :, None]
    halo_ids = jnp.where(place == 0, -1, far_ids[1][:, count - HALO :]) if blocks > 1 else None
    if halo_ids is None:
        halo_ids = jnp.full((rows, HALO), -1, jnp.int32)
    self_ids = jnp.concatenate(
        [jnp.full((rows, count - HALO), -1, jnp.int32), halo_ids, target_segments], axis=1
    )[:, :, None]

    qkv_weight = jnp.concatenate([self_query, self_key, self_value], axis=1)
    kv_weight = jnp.concatenate([cross_key, cross_value], axis=1)

    def ordered(array, chunk):
        mine = lax.dynamic_slice_in_dim(array, chunk * many + core * half, half, 0)
        other = lax.dynamic_slice_in_dim(array, chunk * many + (1 - core) * half, half, 0)
        return mine, other

    def share(mine):
        return jnp.concatenate([mine, send_sibling(mine, lanes)], axis=0)

    def reduced(part_of):
        other = part_of(1)
        return sum_tensor(part_of(0), other, lanes)

    vectors = []
    weights = {}

    def add_weight(name, value):
        weights[name] = weights[name] + value if name in weights else value

    outputs = []
    for chunk in range(CHUNKS):
        own = slice(chunk * many, (chunk + 1) * many)
        target_mine, target_other = ordered(target, chunk)
        tokens = jnp.concatenate([target_mine, target_other], axis=0)
        cotangent, _ = ordered(out_cotangent, chunk)
        ids_here = target_ids[own]
        table_here = table[own]
        source_ids_here = source_ids[own]
        self_ids_here = self_ids[own]
        source_here = source[own]

        qkv = forward_mul(tokens, qkv_weight).astype(bf16)
        halo = send_blk(qkv[:, count - HALO :, width:], 1, blocks)
        self_low, self_sums = self_call(
            False, heads, qkv, halo, (), ids_here[:, :1], self_ids_here, width, shift
        )
        self_halves = halves(self_low)
        first_in = target_mine.astype(f32) + reduced(
            lambda at: forward_mul(self_halves[at], self_output)
        )
        first_unit, first_scale = norm_parts(first_in)
        first = first_unit * first_gain + first_shift
        first_low = share(first.astype(bf16))

        kv = forward_mul(source_here, kv_weight).astype(bf16)
        cross_q = forward_mul(first_low, cross_query).astype(bf16)
        far_q = [cross_q] + [send_blk(cross_q, step, blocks) for step in range(1, blocks)]
        visited = cross_call(
            False, heads, far_q, (), ids_here, source_ids_here, kv, table_here, shift
        )
        back_mixed = [visited[0]] + [
            send_blk(visited[step], -step, blocks) for step in range(1, blocks)
        ]
        back_sums = [visited[blocks]] + [
            send_blk(visited[blocks + step], -step, blocks) for step in range(1, blocks)
        ]
        best = functools.reduce(jnp.maximum, back_sums)
        shares = [jnp.exp2(each - best) for each in back_sums]
        whole = functools.reduce(jnp.add, shares)
        cross_sums = best + jnp.log2(whole)
        cross_mixed = jnp.zeros(cross_q.shape, f32)
        for part, each in zip(back_mixed, shares):
            by_slot = jnp.transpose(each / whole, (0, 2, 1))
            cross_mixed += part.astype(f32) * jnp.repeat(by_slot, HEAD_DIM, axis=2)
        cross_low = cross_mixed.astype(bf16)
        far_sums = [cross_sums] + [send_blk(cross_sums, step, blocks) for step in range(1, blocks)]
        cross_halves = halves(cross_low)
        second_in = first + reduced(lambda at: forward_mul(cross_halves[at], cross_output))
        second_unit, second_scale = norm_parts(second_in)
        second = second_unit * second_gain + second_shift
        second_low = share(second.astype(bf16))

        gate = forward_mul(second_low, ffn_in)
        normal = 0.5 * (1.0 + lax.erf(gate * 0.5**0.5))
        active = (gate * normal).astype(bf16)
        gate_slope = normal + gate * jnp.exp(-0.5 * gate * gate) * 0.3989422804014327
        down = forward_mul(second_low, adapter_down)
        smooth = jax.nn.sigmoid(down)
        rectified = (down * smooth).astype(bf16)
        down_slope = smooth * (1.0 + down * (1.0 - smooth))
        active_halves, rect_halves = halves(active), halves(rectified)
        third_in = second + reduced(
            lambda at: forward_mul(active_halves[at], ffn_out)
            + 4.0 * forward_mul(rect_halves[at], adapter_up)
        )
        third_unit, third_scale = norm_parts(third_in)
        result = (third_unit * third_gain + third_shift).astype(bf16)
        third_grad, third_gain_grad, third_shift_grad = norm_back(
            third_unit, third_scale, third_gain, cotangent.astype(f32)
        )
        branch_grad = share(third_grad.astype(bf16))
        result_other = send_sibling(result, lanes)

        gate_grad = (backward_mul(branch_grad, ffn_out) * gate_slope).astype(bf16)
        down_grad = (4.0 * backward_mul(branch_grad, adapter_up) * down_slope).astype(bf16)
        gate_halves, down_halves = halves(gate_grad), halves(down_grad)
        second_grad = third_grad + reduced(
            lambda at: backward_mul(gate_halves[at], ffn_in)
            + backward_mul(down_halves[at], adapter_down)
        )
        add_weight("adapter_up", 4.0 * weight_mul(rectified, branch_grad))
        add_weight("adapter_down", weight_mul(second_low, down_grad))
        cross_grad, second_gain_grad, second_shift_grad = norm_back(
            second_unit, second_scale, second_gain, second_grad
        )
        cross_branch = share(cross_grad.astype(bf16))

        mixed_grad = backward_mul(cross_branch, cross_output).astype(bf16)
        far_grads = [mixed_grad] + [send_blk(mixed_grad, step, blocks) for step in range(1, blocks)]
        product = mixed_grad.astype(f32) * cross_low.astype(f32)
        delta = jnp.transpose(
            jnp.sum(product.reshape(many, count, heads, HEAD_DIM), axis=-1), (0, 2, 1)
        )
        far_deltas = [delta] + [send_blk(delta, step, blocks) for step in range(1, blocks)]
        visited = cross_call(
            True,
            heads,
            far_q,
            (far_grads, far_sums, far_deltas),
            ids_here,
            source_ids_here,
            kv,
            table_here,
            shift,
        )
        kv_grad = visited[blocks]
        cross_q_sum = visited[0].astype(f32)
        for step in range(1, blocks):
            cross_q_sum += send_blk(visited[step], -step, blocks).astype(f32)
        cross_q_low = cross_q_sum.astype(bf16)
        add_weight("cross_output", weight_mul(cross_low, cross_branch))
        add_weight("cross_kv", weight_mul(source_here, kv_grad))
        source_terms = backward_mul(kv_grad, kv_weight).astype(bf16)
        source_grad = lax.psum_scatter(
            source_terms, "tensor", scatter_dimension=2, tiled=True
        ).astype(f32)
        query_halves = halves(cross_q_low)
        first_grad = cross_grad + reduced(lambda at: backward_mul(query_halves[at], cross_query))
        add_weight("cross_query", weight_mul(first_low, cross_q_low))
        self_grad, first_gain_grad, first_shift_grad = norm_back(
            first_unit, first_scale, first_gain, first_grad
        )
        self_branch = share(self_grad.astype(bf16))

        self_mixed_grad = backward_mul(self_branch, self_output).astype(bf16)
        q_grad, key_own, value_own, side = self_call(
            True,
            heads,
            qkv,
            halo,
            (self_sums, self_mixed_grad),
            ids_here[:, :1],
            self_ids_here,
            width,
            shift,
        )
        side = lax.ppermute(side, "blk", [(i, i - 1) for i in range(1, blocks)]).astype(f32)
        late = ((0, 0), (count - HALO, 0), (0, 0))
        qkv_grad = jnp.concatenate(
            [
                q_grad,
                (key_own + jnp.pad(side[:, :, :width], late)).astype(bf16),
                (value_own + jnp.pad(side[:, :, width:], late)).astype(bf16),
            ],
            axis=2,
        )
        add_weight("self_output", weight_mul(self_low, self_branch))
        add_weight("self_qkv", weight_mul(tokens, qkv_grad))
        qkv_halves = halves(qkv_grad)
        target_grad = self_grad + reduced(lambda at: backward_mul(qkv_halves[at], qkv_weight))
        target_grad_other = send_sibling(target_grad, lanes)
        vectors.append(
            jnp.stack(
                [
                    first_gain_grad,
                    first_shift_grad,
                    second_gain_grad,
                    second_shift_grad,
                    third_gain_grad,
                    third_shift_grad,
                ]
            )
        )
        outputs.append((result, result_other, target_grad, target_grad_other, source_grad))

    result_all = jnp.zeros((rows, count, depth), bf16)
    target_grad_all = jnp.zeros((rows, count, depth), f32)
    for chunk, (result, result_other, mine, other, _) in enumerate(outputs):
        first_at = chunk * many + core * half
        second_at = chunk * many + (1 - core) * half
        result_all = lax.dynamic_update_slice_in_dim(result_all, result, first_at, 0)
        result_all = lax.dynamic_update_slice_in_dim(result_all, result_other, second_at, 0)
        target_grad_all = lax.dynamic_update_slice_in_dim(target_grad_all, mine, first_at, 0)
        target_grad_all = lax.dynamic_update_slice_in_dim(target_grad_all, other, second_at, 0)
    source_grad_all = jnp.concatenate([each[4] for each in outputs], axis=0)

    vector = functools.reduce(jnp.add, vectors)
    vector = vector + send_sibling(vector, lanes)
    portion = depth // lanes
    vector = lax.dynamic_slice_in_dim(vector, lax.axis_index("tensor") * portion, portion, 1)
    vector = lax.psum(vector, ("dp", "blk"))

    def everywhere(value):
        return lax.psum(value.astype(bf16), ("dp", "blk")).astype(f32)

    qkv_sum = everywhere(weights["self_qkv"])
    kv_sum = everywhere(weights["cross_kv"])
    return (
        result_all,
        target_grad_all,
        source_grad_all,
        qkv_sum[:, :width],
        qkv_sum[:, width : 2 * width],
        qkv_sum[:, 2 * width :],
        everywhere(weights["self_output"]),
        everywhere(weights["cross_query"]),
        kv_sum[:, :width],
        kv_sum[:, width:],
        everywhere(weights["cross_output"]),
        everywhere(weights["adapter_down"]),
        everywhere(weights["adapter_up"]),
        vector[0],
        vector[1],
        vector[2],
        vector[3],
        vector[4],
        vector[5],
    )


def solution(mesh):
    return jax.shard_map(
        on_device,
        mesh=mesh,
        in_specs=(
            P("dp", "blk", None),
            P("dp", "blk", None),
            P("dp", "blk"),
            P("dp", "blk"),
            P(None, "tensor"),
            P(None, "tensor"),
            P(None, "tensor"),
            P("tensor", None),
            P(None, "tensor"),
            P(None, "tensor"),
            P(None, "tensor"),
            P("tensor", None),
            P(None, "tensor"),
            P("tensor", None),
            P(None, "tensor"),
            P("tensor", None),
            P(),
            P(),
            P(),
            P(),
            P(),
            P(),
            P("dp", "blk", None),
        ),
        out_specs=(
            P("dp", "blk", None),
            P("dp", "blk", None),
            P("dp", "blk", "tensor"),
            P(None, "tensor"),
            P(None, "tensor"),
            P(None, "tensor"),
            P("tensor", None),
            P(None, "tensor"),
            P(None, "tensor"),
            P(None, "tensor"),
            P("tensor", None),
            P(None, "tensor"),
            P("tensor", None),
            P("tensor"),
            P("tensor"),
            P("tensor"),
            P("tensor"),
            P("tensor"),
            P("tensor"),
        ),
        check_vma=False,
    )
```

```python
import functools

import jax
import jax.numpy as jnp
from jax import lax
from jax.experimental import pallas as pl
from jax.experimental.pallas import tpu as pltpu
from jax.sharding import PartitionSpec as P

HEAD_DIM = 64
HALO = 80
SOURCE_TILE = 512
FFN_TILE = 512
EXTRA = 16
VMEM_LIMIT = 40 * 2**20
VMEM_MOST = 56 * 2**20

epsilon = 1e-05
negative = -1e30
floor = -1e20
log2e = 1.4426950408889634
to_base2 = log2e * HEAD_DIM**-0.5
bf16 = jnp.bfloat16
f32 = jnp.float32


def forward_mul(left, right):
    return jnp.einsum("rti,ij->rtj", left, right, preferred_element_type=f32)


def backward_mul(left, right):
    return jnp.einsum("rtj,ij->rti", left, right, preferred_element_type=f32)


def weight_mul(left, right):
    return jnp.einsum("rti,rtj->ij", left, right, preferred_element_type=f32)


def norm_parts(values):
    centered = values - jnp.mean(values, axis=-1, keepdims=True)
    variance = jnp.mean(centered * centered, axis=-1, keepdims=True)
    scale = lax.rsqrt(variance + epsilon)
    return centered * scale, scale


def norm_back(unit, scale, gain, grad):
    inner = grad * gain
    first = jnp.mean(inner, axis=-1, keepdims=True)
    second = jnp.mean(inner * unit, axis=-1, keepdims=True)
    return (
        scale * (inner - first - unit * second),
        jnp.sum(grad * unit, axis=0),
        jnp.sum(grad, axis=0),
    )


def mul_nt(left, right):
    return lax.dot_general(left, right, (((1,), (1,)), ((), ())), preferred_element_type=f32)


def mul_nn(left, right):
    return lax.dot_general(left, right, (((1,), (0,)), ((), ())), preferred_element_type=f32)


def spread_heads(block, heads):
    if heads == 1:
        return block
    width = block.shape[1]
    lane = lax.broadcasted_iota(jnp.int32, (1, width), 1)
    copies = []
    for head in range(heads):
        inside = (lane >= head * HEAD_DIM) & (lane < (head + 1) * HEAD_DIM)
        copies.append(block * jnp.where(inside, 1.0, 0.0).astype(block.dtype))
    return jnp.concatenate(copies, axis=0)


def tile_lanes(block, heads):
    return jnp.concatenate([block] * heads, axis=1) if heads > 1 else block


def row_of(ref, heads):
    rows = [ref[0, head : head + 1, :] for head in range(heads)]
    return jnp.concatenate(rows, axis=1) if heads > 1 else rows[0]


def store_rows(ref, row, first, heads, count):
    for head in range(heads):
        ref[0, first + head : first + head + 1, :] = row[:, head * count : (head + 1) * count]


def rounded(row):
    return row.astype(bf16).astype(f32)


def pack_rows(ref, lines_ref, rows, width):
    line = 0
    for row in rows:
        for _ in range(3):
            term = rounded(row)
            row = row - term
            for at in range(0, term.shape[1], width):
                lines_ref[line : line + 1, :] = term[:, at : at + width]
                line += 1
    lines_ref[line:, :] = jnp.zeros((EXTRA - line, width), f32)
    ref[0, ref.shape[1] - EXTRA :, :] = lines_ref[...].astype(bf16)


def unpack_rows(ref, lines_ref, total, heads, count):
    width = ref.shape[2]
    lines = heads * count // width
    lines_ref[...] = ref[0, ref.shape[1] - EXTRA :, :].astype(f32)
    rows = []
    for index in range(total):
        pieces = []
        for at in range(lines):
            first = 3 * index * lines + at
            pieces.append(
                lines_ref[first : first + 1, :]
                + lines_ref[first + lines : first + lines + 1, :]
                + lines_ref[first + 2 * lines : first + 2 * lines + 1, :]
            )
        rows.append(jnp.concatenate(pieces, axis=1) if lines > 1 else pieces[0])
    return rows


def head_scale(row, heads, count):
    pieces = [
        jnp.broadcast_to(row[:, head * count : (head + 1) * count], (HEAD_DIM, count))
        for head in range(heads)
    ]
    return jnp.concatenate(pieces, axis=0) if heads > 1 else pieces[0]


def head_products(left, right, heads, count):
    pieces = [
        mul_nn(
            left[head * HEAD_DIM : (head + 1) * HEAD_DIM, :],
            right[:, head * count : (head + 1) * count],
        )
        for head in range(heads)
    ]
    return jnp.concatenate(pieces, axis=0) if heads > 1 else pieces[0]


def cross_forward_kernel(heads, blocks, tile, table_ref, *refs):
    queries = refs[:blocks]
    target_ids, source_ids, keys, values = refs[blocks : blocks + 4]
    mixed = refs[blocks + 4 : 2 * blocks + 4]
    turned, lines, total = refs[2 * blocks + 4 :]
    place = pl.program_id(0)
    count, width = queries[0].shape[1:]
    tiles = keys.shape[1] // tile
    for step in range(tiles):
        turned[step] = values[0, step * tile : (step + 1) * tile, :].T
    for block in range(blocks):
        spread = spread_heads(queries[block][0], heads)
        ids = target_ids[0, block : block + 1, :]
        total[...] = jnp.zeros_like(total)

        def visit(step, carry):
            best, weight = carry
            start = pl.multiple_of(step * tile, tile)
            scores = mul_nt(keys[0, pl.ds(start, tile), :], spread) * to_base2
            allowed = source_ids[0, pl.ds(start, tile), :] == ids
            scores = jnp.where(tile_lanes(allowed, heads), scores, negative)
            fresh = jnp.maximum(best, jnp.max(scores, axis=0, keepdims=True))
            anchor = jnp.maximum(fresh, floor)
            probs = jnp.exp2(scores - anchor)
            fade = jnp.exp2(best - anchor)
            weight = weight * fade + jnp.sum(probs, axis=0, keepdims=True)
            total[...] = total[...] * head_scale(fade, heads, count) + head_products(
                turned[step], probs.astype(bf16), heads, count
            )
            return fresh, weight

        best, weight = lax.fori_loop(
            table_ref[place, 2 * block],
            table_ref[place, 2 * block + 1],
            visit,
            (jnp.full((1, heads * count), negative, f32), jnp.zeros((1, heads * count), f32)),
        )
        some = weight > 0.0
        safe = jnp.where(some, weight, 1.0)
        scaled = total[...] * head_scale(1.0 / safe, heads, count)
        mixed[block][0, :count, :] = scaled.T.astype(bf16)
        sums = jnp.where(some, best + jnp.log2(safe), negative)
        pack_rows(mixed[block], lines.at[block], [sums], width)


def cross_merge_kernel(group, blocks, *refs):
    parts = refs[:blocks]
    weight, mixed, sums, product, lines = refs[blocks:]
    count, width = mixed.shape[1:]
    heads = group // HEAD_DIM
    for index in range(width // group):
        columns = slice(index * group, (index + 1) * group)
        rows = [
            unpack_rows(part.at[:, :, columns], lines.at[at], 1, heads, count)[0]
            for at, part in enumerate(parts)
        ]
        best = functools.reduce(jnp.maximum, rows)
        shares = [jnp.exp2(row - best) for row in rows]
        whole = functools.reduce(jnp.add, shares)
        store_rows(sums, best + jnp.log2(whole), index * heads, heads, count)
        inverse = 1.0 / whole
        total = None
        for part, each in zip(parts, shares):
            scale = head_scale(each * inverse, heads, count).T
            term = part[0, :count, columns].astype(f32) * scale
            total = term if total is None else total + term
        mixed[0, :, columns] = total.astype(bf16)
    product[0] = mul_nn(mixed[0], weight[...])


def cross_prepare_kernel(group, *refs):
    branch, weight, mixed, sums, message, lines = refs
    count, width = mixed.shape[1:]
    heads = group // HEAD_DIM
    grad = mul_nt(branch[0], weight[...]).astype(bf16)
    message[0, :count, :] = grad
    product = (grad.astype(f32) * mixed[0].astype(f32)).T
    for index in range(width // group):
        columns = slice(index * group, (index + 1) * group)
        delta, offset = [], []
        for head in range(index * heads, (index + 1) * heads):
            delta.append(
                jnp.sum(product[head * HEAD_DIM : (head + 1) * HEAD_DIM], axis=0, keepdims=True)
            )
            offset.append(sums[0, head : head + 1, :])
        if heads > 1:
            delta, offset = [jnp.concatenate(delta, axis=1)], [jnp.concatenate(offset, axis=1)]
        pack_rows(message.at[:, :, columns], lines, [offset[0], delta[0]], group)


def cross_backward_kernel(heads, blocks, tile, table_ref, *refs):
    queries = refs[:blocks]
    grads = refs[blocks : 2 * blocks]
    target_ids, source_ids, keys, values = refs[2 * blocks : 2 * blocks + 4]
    query_grads = refs[2 * blocks + 4 : 3 * blocks + 4]
    source_side, turned, lines, key_grad, value_grad, total = refs[3 * blocks + 4 :]
    place = pl.program_id(0)
    count, width = queries[0].shape[1:]
    tiles = keys.shape[1] // tile
    for step in range(tiles):
        turned[step] = keys[0, step * tile : (step + 1) * tile, :].T
    key_grad[...] = jnp.zeros_like(key_grad)
    value_grad[...] = jnp.zeros_like(value_grad)
    for block in range(blocks):
        spread = spread_heads(queries[block][0], heads)
        spread_grad = spread_heads(grads[block][0, :count, :], heads)
        offset, delta = unpack_rows(grads[block], lines.at[block], 2, heads, count)
        ids = target_ids[0, block : block + 1, :]
        total[...] = jnp.zeros_like(total)

        def visit(step, carry):
            start = pl.multiple_of(step * tile, tile)
            span = pl.ds(start, tile)
            scores = mul_nt(keys[0, span, :], spread) * to_base2
            allowed = source_ids[0, span, :] == ids
            probs = jnp.where(tile_lanes(allowed, heads), jnp.exp2(scores - offset), 0.0)
            dprobs = mul_nt(values[0, span, :], spread_grad)
            dscores = (probs * (dprobs - delta)).astype(bf16)
            key_grad[span, :] += mul_nn(dscores, spread)
            value_grad[span, :] += mul_nn(probs.astype(bf16), spread_grad)
            total[...] += head_products(turned[step], dscores, heads, count)
            return carry

        lax.fori_loop(table_ref[place, 2 * block], table_ref[place, 2 * block + 1], visit, 0)
        query_grads[block][0] = (total[...] * HEAD_DIM**-0.5).T.astype(bf16)
    source_side[0] = jnp.concatenate(
        [(key_grad[...] * HEAD_DIM**-0.5).astype(bf16), value_grad[...].astype(bf16)], axis=1
    )


def self_scores(heads, queries, keys, source_ids, ids):
    spread = spread_heads(queries, heads)
    scores = mul_nt(keys, spread) * to_base2
    count = queries.shape[0]
    slots = keys.shape[0]
    key_place = lax.broadcasted_iota(jnp.int32, (slots, count), 0) - (slots - count)
    query_place = lax.broadcasted_iota(jnp.int32, (slots, count), 1)
    allowed = (source_ids == ids) & (key_place <= query_place)
    return spread, scores, tile_lanes(allowed, heads)


def with_halo(halo, own):
    missing = own.shape[0] - halo.shape[0]
    return jnp.concatenate([jnp.zeros((missing, own.shape[1]), own.dtype), halo, own], axis=0)


def self_forward_kernel(heads, *refs):
    queries, keys, values, key_halo, value_halo, target_ids, source_ids, mixed, sums = refs
    count = queries.shape[1]
    every_key = with_halo(key_halo[0], keys[0])
    every_value = with_halo(value_halo[0], values[0])
    _, scores, allowed = self_scores(
        heads, queries[0], every_key, source_ids[0], target_ids[0, 0:1, :]
    )
    scores = jnp.where(allowed, scores, negative)
    best = jnp.max(scores, axis=0, keepdims=True)
    probs = jnp.exp2(scores - best)
    weight = jnp.sum(probs, axis=0, keepdims=True)
    total = head_products(every_value.T, probs.astype(bf16), heads, count)
    mixed[0] = (total * head_scale(1.0 / weight, heads, count)).T.astype(bf16)
    store_rows(sums, best + jnp.log2(weight), 0, heads, count)


def self_backward_kernel(heads, *refs):
    queries, keys, values, key_halo, value_halo, target_ids, source_ids, sums, grads = refs[:9]
    query_grad, key_own, value_own, side = refs[9:]
    count = queries.shape[1]
    every_key = with_halo(key_halo[0], keys[0])
    every_value = with_halo(value_halo[0], values[0])
    spread, scores, allowed = self_scores(
        heads, queries[0], every_key, source_ids[0], target_ids[0, 0:1, :]
    )
    spread_grad = spread_heads(grads[0], heads)
    probs = jnp.where(allowed, jnp.exp2(scores - row_of(sums, heads)), 0.0)
    dprobs = mul_nt(every_value, spread_grad)
    delta = jnp.sum(probs * dprobs, axis=0, keepdims=True)
    dscores = (probs * (dprobs - delta)).astype(bf16)
    key_grad = mul_nn(dscores, spread) * HEAD_DIM**-0.5
    value_grad = mul_nn(probs.astype(bf16), spread_grad)
    total = head_products(every_key.T, dscores, heads, count)
    query_grad[0] = (total * HEAD_DIM**-0.5).T.astype(bf16)
    slots = every_key.shape[0]
    first = slots - count - HALO
    key_own[0] = key_grad[slots - count :, :]
    value_own[0] = value_grad[slots - count :, :]
    side[0] = jnp.concatenate(
        [
            key_grad[first : slots - count, :].astype(bf16),
            value_grad[first : slots - count, :].astype(bf16),
        ],
        axis=1,
    )


def group_width(width, total):
    return width if width % 128 == 0 else total


def cross_call(backward, group, queries, grads, target_ids, source_ids, kv, table):
    blocks = len(queries)
    rows, count, width = queries[0].shape
    slots = kv.shape[1]
    tile = min(SOURCE_TILE, slots)
    heads = group // HEAD_DIM
    token = pl.BlockSpec((1, count, group), lambda i, g, t: (i, 0, g))
    packed = pl.BlockSpec((1, count + EXTRA, group), lambda i, g, t: (i, 0, g))
    in_specs = [token] * blocks
    operands = list(queries)
    if backward:
        in_specs += [packed] * blocks
        operands += list(grads)
    in_specs += [
        pl.BlockSpec((1, blocks, count), lambda i, g, t: (i, 0, 0)),
        pl.BlockSpec((1, slots, 1), lambda i, g, t: (i, 0, 0)),
        pl.BlockSpec((1, slots, group), lambda i, g, t: (i, 0, 2 * g)),
        pl.BlockSpec((1, slots, group), lambda i, g, t: (i, 0, 2 * g + 1)),
    ]
    operands += [target_ids, source_ids, kv, kv]
    scratch = [
        pltpu.VMEM((slots // tile, group, tile), bf16),
        pltpu.VMEM((blocks, EXTRA, group), f32),
    ]
    if backward:
        out_shape = [jax.ShapeDtypeStruct((rows, count, width), bf16)] * blocks
        out_shape += [jax.ShapeDtypeStruct((rows, slots, 2 * width), bf16)]
        out_specs = [token] * blocks + [
            pl.BlockSpec((1, slots, 2 * group), lambda i, g, t: (i, 0, g))
        ]
        scratch += [pltpu.VMEM((slots, group), f32), pltpu.VMEM((slots, group), f32)]
    else:
        out_shape = [jax.ShapeDtypeStruct((rows, count + EXTRA, width), bf16)] * blocks
        out_specs = [packed] * blocks
    scratch += [pltpu.VMEM((group, count), f32)]
    work = rows * slots * blocks * count * width // 2
    return pl.pallas_call(
        functools.partial(
            cross_backward_kernel if backward else cross_forward_kernel, heads, blocks, tile
        ),
        grid_spec=pltpu.PrefetchScalarGridSpec(
            num_scalar_prefetch=1,
            grid=(rows, width // group),
            in_specs=in_specs,
            out_specs=out_specs,
            scratch_shapes=scratch,
        ),
        out_shape=out_shape,
        compiler_params=pltpu.CompilerParams(vmem_limit_bytes=VMEM_MOST),
        cost_estimate=pl.CostEstimate(
            flops=work * (20 if backward else 8),
            bytes_accessed=rows * slots * width * (8 if backward else 4),
            transcendentals=0,
        ),
        name="cross_backward" if backward else "cross_forward",
    )(table, *operands)


def merge_call(group, parts, weight):
    rows, tall, width = parts[0].shape
    count = tall - EXTRA
    depth = weight.shape[1]
    heads = width // HEAD_DIM
    return pl.pallas_call(
        functools.partial(cross_merge_kernel, group, len(parts)),
        grid=(rows,),
        in_specs=[pl.BlockSpec((1, tall, width), lambda i: (i, 0, 0))] * len(parts)
        + [pl.BlockSpec(weight.shape, lambda i: (0, 0))],
        out_specs=[
            pl.BlockSpec((1, count, width), lambda i: (i, 0, 0)),
            pl.BlockSpec((1, heads, count), lambda i: (i, 0, 0)),
            pl.BlockSpec((1, count, depth), lambda i: (i, 0, 0)),
        ],
        out_shape=[
            jax.ShapeDtypeStruct((rows, count, width), bf16),
            jax.ShapeDtypeStruct((rows, heads, count), f32),
            jax.ShapeDtypeStruct((rows, count, depth), f32),
        ],
        scratch_shapes=[pltpu.VMEM((len(parts), EXTRA, group), f32)],
        compiler_params=pltpu.CompilerParams(vmem_limit_bytes=VMEM_LIMIT),
        cost_estimate=pl.CostEstimate(
            flops=2 * rows * count * width * depth,
            bytes_accessed=rows * tall * (width * 8 + depth * 4),
            transcendentals=0,
        ),
        name="cross_merge",
    )(*parts, weight)


def prepare_call(group, branch, weight, mixed, sums):
    rows, count, width = mixed.shape
    depth = branch.shape[2]
    heads = width // HEAD_DIM
    return pl.pallas_call(
        functools.partial(cross_prepare_kernel, group),
        grid=(rows,),
        in_specs=[
            pl.BlockSpec((1, count, depth), lambda i: (i, 0, 0)),
            pl.BlockSpec(weight.shape, lambda i: (0, 0)),
            pl.BlockSpec((1, count, width), lambda i: (i, 0, 0)),
            pl.BlockSpec((1, heads, count), lambda i: (i, 0, 0)),
        ],
        out_specs=pl.BlockSpec((1, count + EXTRA, width), lambda i: (i, 0, 0)),
        out_shape=jax.ShapeDtypeStruct((rows, count + EXTRA, width), bf16),
        scratch_shapes=[pltpu.VMEM((EXTRA, group), f32)],
        compiler_params=pltpu.CompilerParams(vmem_limit_bytes=VMEM_LIMIT),
        cost_estimate=pl.CostEstimate(
            flops=2 * rows * count * width * depth,
            bytes_accessed=rows * count * (width * 6 + depth * 2),
            transcendentals=0,
        ),
        name="cross_prepare",
    )(branch, weight, mixed, sums)


def mul_tn(left, right):
    return lax.dot_general(left, right, (((0,), (0,)), ((), ())), preferred_element_type=f32)


def project_kernel(row, tokens, weight, out):
    out[0] = mul_nn(tokens[0], weight[...]).astype(bf16)


def source_weight_kernel(row, tokens, grad, total):
    @pl.when((pl.program_id(0) == 0) & (pl.program_id(1) == 0))
    def _():
        total[...] = jnp.zeros_like(total)

    total[...] += mul_tn(tokens[0], grad[0])


def source_other_kernel(grad, weight, out):
    out[0] = mul_nt(grad[0], weight[...]).astype(bf16)


def source_own_kernel(grad, weight, across, own, peer):
    width = own.shape[2]
    total = mul_nt(grad[0], weight[...]) + across[0].astype(f32)
    own[0] = total[:, :width]
    peer[0] = total[:, width:].astype(bf16)


def source_call(kernel, row, rows, slots, operands, blocks, outs, name):
    tile = min(FFN_TILE, slots)
    prefetch = row is not None

    def spec(shape, kind):
        if kind == "all":
            return pl.BlockSpec(shape, lambda i, j, *r: (0, 0))
        if kind == "far":
            return pl.BlockSpec((1, tile, shape[2]), lambda i, j, r: (r[0] + i, j, 0))
        return pl.BlockSpec((1, tile, shape[2]), lambda i, j, *r: (i, j, 0))

    count = len(operands)
    return pl.pallas_call(
        kernel,
        grid_spec=pltpu.PrefetchScalarGridSpec(
            num_scalar_prefetch=1 if prefetch else 0,
            grid=(rows, slots // tile),
            in_specs=[spec(each.shape, kind) for each, kind in zip(operands, blocks)],
            out_specs=[spec(each.shape, kind) for each, kind in zip(outs, blocks[count:])],
        ),
        out_shape=outs,
        compiler_params=pltpu.CompilerParams(vmem_limit_bytes=VMEM_MOST),
        cost_estimate=pl.CostEstimate(flops=0, bytes_accessed=0, transcendentals=0),
        name=name,
    )(*([row] if prefetch else []), *operands)


def ffn_forward_kernel(tokens, weight_in, weight_out, down, up, total, slope, rect, down_slope):
    @pl.when(pl.program_id(0) == 0)
    def _():
        value = mul_nn(tokens[...], down[...])
        smooth = 1.0 / (1.0 + jnp.exp(-value))
        low = (value * smooth).astype(bf16)
        rect[...] = low
        down_slope[...] = smooth * (1.0 + value * (1.0 - smooth))
        total[...] = 4.0 * mul_nn(low, up[...])

    gate = mul_nn(tokens[...], weight_in[...])
    normal = 0.5 * (1.0 + lax.erf(gate * 0.5**0.5))
    slope[...] = (normal + gate * jnp.exp(-0.5 * gate * gate) * 0.3989422804014327).astype(bf16)
    total[...] += mul_nn((gate * normal).astype(bf16), weight_out[...])


def ffn_backward_kernel(grad, weight_in, weight_out, down, up, slope, down_slope, total, down_grad):
    @pl.when(pl.program_id(0) == 0)
    def _():
        low = (4.0 * mul_nt(grad[...], up[...]) * down_slope[...]).astype(bf16)
        down_grad[...] = low
        total[...] = mul_nt(low, down[...])

    gate_grad = (mul_nt(grad[...], weight_out[...]) * slope[...].astype(f32)).astype(bf16)
    total[...] += mul_nt(gate_grad, weight_in[...])


def ffn_call(backward, tokens, weight_in, weight_out, down, up, slopes=()):
    count, depth = tokens.shape
    hidden = weight_in.shape[1]
    extra = down.shape[1]
    tile = min(FFN_TILE, hidden)
    whole = lambda shape: pl.BlockSpec(shape, lambda j: (0, 0))
    across = pl.BlockSpec((count, tile), lambda j: (0, j))
    in_specs = [
        whole((count, depth)),
        pl.BlockSpec((depth, tile), lambda j: (0, j)),
        pl.BlockSpec((tile, depth), lambda j: (j, 0)),
        whole((depth, extra)),
        whole((extra, depth)),
    ]
    out_shape = [jax.ShapeDtypeStruct((count, depth), f32)]
    out_specs = [whole((count, depth))]
    if backward:
        in_specs += [across, whole((count, extra))]
        out_shape += [jax.ShapeDtypeStruct((count, extra), bf16)]
        out_specs += [whole((count, extra))]
    else:
        out_shape += [
            jax.ShapeDtypeStruct((count, hidden), bf16),
            jax.ShapeDtypeStruct((count, extra), bf16),
            jax.ShapeDtypeStruct((count, extra), f32),
        ]
        out_specs += [across, whole((count, extra)), whole((count, extra))]
    return pl.pallas_call(
        ffn_backward_kernel if backward else ffn_forward_kernel,
        grid=(hidden // tile,),
        in_specs=in_specs,
        out_specs=out_specs,
        out_shape=out_shape,
        compiler_params=pltpu.CompilerParams(vmem_limit_bytes=VMEM_LIMIT),
        cost_estimate=pl.CostEstimate(
            flops=4 * count * hidden * depth,
            bytes_accessed=4 * hidden * depth,
            transcendentals=0,
        ),
        name="ffn_backward" if backward else "ffn_forward",
    )(tokens, weight_in, weight_out, down, up, *slopes)


def self_call(backward, group, qkv, halo, extra, target_ids, source_ids):
    rows, count = qkv.shape[:2]
    width = qkv.shape[2] // 3
    groups = width // group
    heads = group // HEAD_DIM
    in_specs = [
        pl.BlockSpec((1, count, group), lambda i, g, at=at: (i, 0, 3 * g + at)) for at in range(3)
    ]
    in_specs += [
        pl.BlockSpec((1, HALO, group), lambda i, g, at=at: (i, 0, 2 * g + at)) for at in range(2)
    ]
    token = pl.BlockSpec((1, count, group), lambda i, g: (i, 0, g))
    stat = pl.BlockSpec((1, None, heads, count), lambda i, g: (i, g, 0, 0))
    in_specs += [
        pl.BlockSpec((1, 1, count), lambda i, g: (i, 0, 0)),
        pl.BlockSpec((1, 2 * count, 1), lambda i, g: (i, 0, 0)),
    ]
    operands = [qkv, qkv, qkv, halo, halo, target_ids, source_ids]
    token_shape = (rows, count, width)
    if backward:
        in_specs += [stat, token]
        operands += list(extra)
        out_shape = [
            jax.ShapeDtypeStruct(token_shape, bf16),
            jax.ShapeDtypeStruct(token_shape, f32),
            jax.ShapeDtypeStruct(token_shape, f32),
            jax.ShapeDtypeStruct((rows, HALO, 2 * width), bf16),
        ]
        out_specs = [
            token,
            token,
            token,
            pl.BlockSpec((1, HALO, 2 * group), lambda i, g: (i, 0, g)),
        ]
    else:
        out_shape = [
            jax.ShapeDtypeStruct(token_shape, bf16),
            jax.ShapeDtypeStruct((rows, groups, heads, count), f32),
        ]
        out_specs = [token, stat]
    work = rows * count * count * width
    return pl.pallas_call(
        functools.partial(self_backward_kernel if backward else self_forward_kernel, heads),
        grid=(rows, groups),
        in_specs=in_specs,
        out_specs=out_specs,
        out_shape=out_shape,
        compiler_params=pltpu.CompilerParams(vmem_limit_bytes=VMEM_LIMIT),
        cost_estimate=pl.CostEstimate(
            flops=work * (40 if backward else 16),
            bytes_accessed=rows * count * width * 12,
            transcendentals=0,
        ),
        name="self_backward" if backward else "self_forward",
    )(*operands)


def send_blk(array, distance, size):
    return lax.ppermute(array, "blk", [(i, (i + distance) % size) for i in range(size)])


def send_sibling(array, size):
    return lax.ppermute(array, "tensor", [(i, i ^ 1) for i in range(size)])


def send_outer(array, distance, size):
    return lax.ppermute(array, "tensor", [(i, (i + 2 * distance) % size) for i in range(size)])


def tie(token, *arrays):
    if token is None:
        return arrays
    return lax.optimization_barrier((token, *arrays))[1:]


def sum_grid(value, first=(), others_of=lambda first: ()):
    groups, blocks = lax.axis_size("dp"), lax.axis_size("blk")
    group, place = lax.axis_index("dp"), lax.axis_index("blk")
    depth, width = value.shape

    def send_dp(array, step):
        return lax.ppermute(array, "dp", [(i, (i + step) % groups) for i in range(groups)])

    def reduce_over(array, index, size, send):
        many = array.shape[0] // size
        mine = lax.dynamic_slice_in_dim(array, index * many, many, 0)
        for step in range(1, size):
            to = lax.rem(index + step, size)
            other = lax.dynamic_slice_in_dim(array, to * many, many, 0)
            mine = mine + send(other.astype(bf16), step).astype(f32)
        return mine

    def gather_over(array, index, size, send):
        many = array.shape[0]
        whole = jnp.zeros((many * size, width), array.dtype)
        whole = lax.dynamic_update_slice_in_dim(whole, array, index * many, 0)
        for step in range(1, size):
            source = lax.rem(index - step + size, size)
            whole = lax.dynamic_update_slice_in_dim(whole, send(array, step), source * many, 0)
        return whole

    def over_blk(array, step):
        return send_blk(array, step, blocks)

    total = reduce_over(value, group, groups, send_dp)
    total, first = lax.optimization_barrier((total, first))
    others = others_of(first)
    total = reduce_over(total, place, blocks, over_blk).astype(bf16)
    total = gather_over(total, place, blocks, over_blk)
    total, others = lax.optimization_barrier((total, others))
    return gather_over(total, group, groups, send_dp), others


def sum_small(value):
    groups, blocks = lax.axis_size("dp"), lax.axis_size("blk")
    total = value
    for step in range(1, groups):
        total = total + lax.ppermute(
            value, "dp", [(i, (i + step) % groups) for i in range(groups)]
        )
    value = total
    for step in range(1, blocks):
        total = total + send_blk(value, step, blocks)
    return total


def on_device(
    target,
    source,
    target_segments,
    source_segments,
    self_query,
    self_key,
    self_value,
    self_output,
    cross_query,
    cross_key,
    cross_value,
    cross_output,
    ffn_in,
    ffn_out,
    adapter_down,
    adapter_up,
    first_gain,
    first_shift,
    second_gain,
    second_shift,
    third_gain,
    third_shift,
    out_cotangent,
):
    rows, count, depth = target.shape
    slots = source.shape[1]
    width = self_query.shape[1]
    extra = adapter_up.shape[0]
    blocks = lax.axis_size("blk")
    lanes = lax.axis_size("tensor")
    place = lax.axis_index("blk")
    lane = lax.axis_index("tensor")
    core = lax.rem(lane, 2)
    chip = lane // 2
    chips = lanes // 2
    many = rows // chips
    half = many * count // 2
    tile = min(SOURCE_TILE, slots)
    wide = width * chips
    group = group_width(width, wide)
    groups = range(wide // group)

    def over_blk(array):
        return [array] + [send_blk(array, step, blocks) for step in range(1, blocks)]

    def back_blk(arrays):
        return [arrays[0]] + [send_blk(arrays[step], -step, blocks) for step in range(1, blocks)]

    def over_chips(array):
        return [array] + [send_outer(array, step, lanes) for step in range(1, chips)]

    def home_chips(arrays):
        total = arrays[0]
        for step in range(1, chips):
            total = total + send_outer(arrays[step].astype(bf16), -step, lanes).astype(f32)
        return total

    def packed_over_chips(*arrays):
        flat = jnp.concatenate([each.reshape(-1, depth) for each in arrays], axis=0)
        lists = [[each] for each in arrays]
        for step in range(1, chips):
            far = send_outer(flat, step, lanes)
            at = 0
            for each, gathered in zip(arrays, lists):
                size = each.size // depth
                gathered.append(far[at : at + size].reshape(each.shape))
                at += size
        return lists

    def chip_rows(array, step):
        at = lax.rem(chip + step, chips) * many
        return lax.dynamic_slice_in_dim(array, at, many, 0)

    def core_half(array):
        flat = array.reshape(many * count, array.shape[-1])
        return lax.dynamic_slice_in_dim(flat, core * half, half, 0)

    def share(mine):
        other = send_sibling(mine, lanes)
        first_one = core == 0
        both = [jnp.where(first_one, mine, other), jnp.where(first_one, other, mine)]
        return jnp.concatenate(both, axis=0).reshape(many, count, mine.shape[-1])

    def reduced(part):
        flat = part.reshape(many * count, part.shape[-1])
        other = lax.dynamic_slice_in_dim(flat, (1 - core) * half, half, 0).astype(bf16)
        return core_half(part) + send_sibling(other, lanes).astype(f32)

    def total_of(multiply, lefts, rights):
        return functools.reduce(jnp.add, [multiply(a, b) for a, b in zip(lefts, rights)])

    def by_group(*lists):
        joined = [jnp.concatenate(each, axis=-1) for each in lists]
        pieces = [
            each[..., at * group : (at + 1) * group] for at in groups for each in joined
        ]
        return jnp.concatenate(pieces, axis=-1)

    def ungroup(array, kinds):
        return [
            jnp.concatenate(
                [
                    array[..., (at * kinds + kind) * group : (at * kinds + kind + 1) * group]
                    for at in groups
                ],
                axis=-1,
            )
            for kind in range(kinds)
        ]

    def lane_columns(array):
        return [array[..., at * width : (at + 1) * width] for at in range(chips)]

    far_ids = over_blk(chip_rows(target_segments, 0))
    target_ids = jnp.stack(far_ids, axis=1)
    first_row = (chip * many).astype(jnp.int32).reshape(1)
    source_segments = chip_rows(source_segments, 0)
    tiles = source_segments.reshape(many, slots // tile, tile)
    table = jnp.stack(
        [
            jnp.sum(tiles[:, None, :, -1] < target_ids[:, :, :1], axis=-1, dtype=jnp.int32),
            jnp.sum(tiles[:, None, :, 0] <= target_ids[:, :, -1:], axis=-1, dtype=jnp.int32),
        ],
        axis=-1,
    ).reshape(many, 2 * blocks)
    source_ids = source_segments[:, :, None]
    halo_ids = jnp.where(place == 0, -1, far_ids[-1 + min(blocks, 2)][:, count - HALO :])
    self_ids = jnp.concatenate(
        [jnp.full((many, count - HALO), -1, jnp.int32), halo_ids, far_ids[0]], axis=1
    )[:, :, None]
    own_ids = target_ids[:, :1]

    qkv_weight = jnp.concatenate([self_query, self_key, self_value], axis=1)
    all_tokens = jnp.concatenate([chip_rows(target, step) for step in range(chips)], axis=0)
    tokens = all_tokens[:many]
    target_mine = core_half(tokens)
    flat_cotangent = out_cotangent.reshape(rows * count, depth)
    cotangent = lax.dynamic_slice_in_dim(
        flat_cotangent, chip * many * count + core * half, half, 0
    )
    self_outputs = over_chips(self_output)
    every = forward_mul(all_tokens, qkv_weight).astype(bf16)
    qkv = [every[:many]] + [
        send_outer(every[step * many : (step + 1) * many], step, lanes)
        for step in range(1, chips)
    ]
    arrived = qkv[-1]
    qkv = by_group(*[[each[..., at * width : (at + 1) * width] for each in qkv] for at in range(3)])
    halo = jnp.concatenate(
        [
            qkv[:, count - HALO :, (3 * at + 1) * group : (3 * at + 3) * group]
            for at in groups
        ],
        axis=2,
    )
    halo = send_blk(halo, 1, blocks)
    cross_queries = over_chips(tie(arrived, cross_query)[0])
    halo, cross_queries, self_outputs = lax.optimization_barrier(
        (halo, cross_queries, self_outputs)
    )

    self_low, self_sums = self_call(False, group, qkv, halo, (), own_ids, self_ids)
    self_outputs = jnp.concatenate(self_outputs, axis=0)
    first_in = target_mine.astype(f32) + reduced(forward_mul(self_low, self_outputs))
    first_unit, first_scale = norm_parts(first_in)
    first = first_unit * first_gain + first_shift
    first_low = share(first.astype(bf16))

    cross_queries = jnp.concatenate(cross_queries, axis=1)
    cross_q = forward_mul(first_low, cross_queries).astype(bf16)
    far_q = over_blk(cross_q)
    near_kv = tie(cross_q, jnp.concatenate([cross_key, cross_value], axis=1))[0]
    kv_weights = over_chips(near_kv)
    kv_weight = by_group(
        [each[:, :width] for each in kv_weights], [each[:, width:] for each in kv_weights]
    )
    (kv,) = source_call(
        project_kernel,
        first_row,
        many,
        slots,
        (source, kv_weight),
        ("far", "all", "near"),
        [jax.ShapeDtypeStruct((many, slots, 2 * wide), bf16)],
        "source_project",
    )
    near = tie(kv_weights[-1], cross_output, ffn_in, adapter_down)
    cross_outputs, ffn_ins = packed_over_chips(*near[:2])
    downs = over_chips(near[2])
    visited = cross_call(False, group, far_q, (), target_ids, source_ids, kv, table)
    back = back_blk(visited)
    ffn_outs, ups = packed_over_chips(*tie(visited[0], ffn_out, adapter_up))
    back, cross_outputs, ffn_ins, downs = lax.optimization_barrier(
        (back, cross_outputs, ffn_ins, downs)
    )
    cross_outputs = jnp.concatenate(cross_outputs, axis=0)
    down_weight = jnp.concatenate(downs, axis=1)
    ffn_in_weight = jnp.concatenate(ffn_ins, axis=1)
    ffn_out_weight = jnp.concatenate(ffn_outs, axis=0)
    up_weight = jnp.concatenate(ups, axis=0)
    cross_low, cross_sums, branch = merge_call(group, back, cross_outputs)
    second_in = first + reduced(branch)
    second_unit, second_scale = norm_parts(second_in)
    second = second_unit * second_gain + second_shift
    second_low = share(second.astype(bf16))

    ffn_weights = (ffn_in_weight, ffn_out_weight, down_weight, up_weight)
    branch, gate_slope, rectified, down_slope = ffn_call(
        False, second_low.reshape(many * count, depth), *ffn_weights
    )
    third_in = second + reduced(branch)
    third_unit, third_scale = norm_parts(third_in)
    result = (third_unit * third_gain + third_shift).astype(bf16)
    third_grad, third_gain_grad, third_shift_grad = norm_back(
        third_unit, third_scale, third_gain, cotangent.astype(f32)
    )
    branch_grad = share(third_grad.astype(bf16))

    branch, down_grad = ffn_call(
        True, branch_grad.reshape(many * count, depth), *ffn_weights, (gate_slope, down_slope)
    )
    second_grad = third_grad + reduced(branch)
    cross_grad, second_gain_grad, second_shift_grad = norm_back(
        second_unit, second_scale, second_gain, second_grad
    )
    cross_branch = share(cross_grad.astype(bf16))

    message = prepare_call(group, cross_branch, cross_outputs, cross_low, cross_sums)
    far_grads = over_blk(message)
    early = [
        jnp.concatenate(
            [
                4.0 * weight_mul(branch_grad, up),
                weight_mul(second_low, down),
                weight_mul(cross_branch, low),
            ],
            axis=1,
        )
        for up, down, low in zip(
            *[
                [
                    each.reshape(many, count, -1)[..., at * extra : (at + 1) * extra]
                    for at in range(chips)
                ]
                for each in (rectified, down_grad)
            ],
            lane_columns(cross_low),
        )
    ]
    early = home_chips(early)
    results = over_chips(tie(message, result)[0])
    far_grads, early, results = lax.optimization_barrier((far_grads, early, results))
    visited = cross_call(True, group, far_q, far_grads, target_ids, source_ids, kv, table)
    kv_grad = visited[blocks]
    back = back_blk(visited[:blocks])
    qkv_weights = over_chips(tie(kv_grad, qkv_weight)[0])
    (kv_grad_now,) = tie(back[min(1, blocks - 1)], kv_grad)

    def owner_rows(parity):
        owners = [lax.rem(chip + step, chips) * 2 + parity for step in range(chips)]
        rows_of = [
            lax.dynamic_slice_in_dim(kv_weight, owner * width, width, 0) for owner in owners
        ]
        return jnp.concatenate(rows_of, axis=0)

    (kv_weight_grad,) = source_call(
        source_weight_kernel,
        first_row,
        many,
        slots,
        (source, kv_grad_now),
        ("far", "near", "all"),
        [jax.ShapeDtypeStruct((depth, 2 * wide), f32)],
        "source_weight",
    )
    middle = [
        jnp.concatenate(each, axis=1)
        for each in zip(*[lane_columns(each) for each in ungroup(kv_weight_grad, 2)])
    ]
    (across,) = source_call(
        source_other_kernel,
        None,
        many,
        slots,
        (kv_grad_now, owner_rows(1 - core)),
        ("near", "all", "near"),
        [jax.ShapeDtypeStruct((many, slots, wide), bf16)],
        "source_other",
    )
    back, qkv_weights, middle, across = lax.optimization_barrier(
        (back, qkv_weights, middle, across)
    )
    cross_q_low = functools.reduce(jnp.add, [part.astype(f32) for part in back]).astype(bf16)
    first_grad = cross_grad + reduced(backward_mul(cross_q_low, cross_queries))
    self_grad, first_gain_grad, first_shift_grad = norm_back(
        first_unit, first_scale, first_gain, first_grad
    )
    middle = home_chips(list(tie(cross_q_low, *middle)))
    self_branch = share(self_grad.astype(bf16))

    mixed_grad = backward_mul(self_branch, self_outputs).astype(bf16)
    q_grad, key_own, value_own, side = self_call(
        True, group, qkv, halo, (self_sums, mixed_grad), own_ids, self_ids
    )
    side = lax.ppermute(side, "blk", [(i, i - 1) for i in range(1, blocks)])
    (middle,) = tie(q_grad, jnp.concatenate([early, middle], axis=1).astype(bf16))
    middle = lax.psum(middle, ("dp", "blk"))
    across = send_sibling(across, lanes)
    vector = jnp.stack(
        [
            first_gain_grad,
            first_shift_grad,
            second_gain_grad,
            second_shift_grad,
            third_gain_grad,
            third_shift_grad,
        ]
    )
    portion = depth // lanes
    lines = 6 * portion // (2 * width)
    below = 16 * lax.axis_size("dp") * blocks

    def vector_rows(step):
        owner = lax.rem(chip - step + chips, chips) * 2 + core
        piece = lax.dynamic_slice_in_dim(vector, owner * portion, portion, 1)
        return jnp.pad(piece.reshape(lines, 2 * width), ((0, below - lines), (0, 0)))

    vector, late_branch, late_low = tie(q_grad, vector, self_branch, first_low)
    vector = vector + send_sibling(vector, lanes)
    late = [
        jnp.concatenate([jnp.concatenate(each, axis=1), vector_rows(step)], axis=0)
        for step, each in enumerate(
            zip(
                lane_columns(weight_mul(late_branch, self_low)),
                lane_columns(weight_mul(late_low, cross_q_low)),
            )
        )
    ]
    late = home_chips(late)
    after = ((0, 0), (count - HALO, 0), (0, 0))
    key_side, value_side = [jnp.pad(each.astype(f32), after) for each in ungroup(side, 2)]
    key_grad = (key_own + key_side).astype(bf16)
    value_grad = (value_own + value_side).astype(bf16)
    qkv_grad = [
        jnp.concatenate(each, axis=2)
        for each in zip(lane_columns(q_grad), lane_columns(key_grad), lane_columns(value_grad))
    ]
    home = [qkv_grad[0]] + [
        send_outer(qkv_grad[step], -step, lanes) for step in range(1, chips)
    ]
    self_qkv_grad = weight_mul(all_tokens, jnp.concatenate(home, axis=0))
    source_own, source_peer = source_call(
        source_own_kernel,
        None,
        many,
        slots,
        (tie(home[-1], kv_grad)[0], owner_rows(core), across),
        ("near", "all", "near", "near", "near"),
        [
            jax.ShapeDtypeStruct((many, slots, width), f32),
            jax.ShapeDtypeStruct((many, slots, wide - width), bf16),
        ],
        "source_own",
    )

    def source_sends(first):
        own, peer = first
        far = [
            send_outer(peer[:, :, (step - 1) * width : step * width], step, lanes)
            for step in range(1, chips)
        ]
        return middle, [own] + far

    late, (middle, source_parts) = sum_grid(
        tie(self_qkv_grad, late)[0], (source_own, source_peer), source_sends
    )
    (self_grad, *qkv_grad) = tie(self_qkv_grad, self_grad, *qkv_grad)
    target_grad = self_grad + reduced(total_of(backward_mul, qkv_grad, qkv_weights))
    target_grads = over_chips(lax.optimization_barrier(target_grad.astype(bf16)))

    def everywhere(pieces, dtype):
        whole = jnp.zeros((rows * count, depth), dtype)
        for step, piece in enumerate(pieces):
            first_at = lax.rem(chip - step + chips, chips) * many * count
            other = send_sibling(piece, lanes)
            whole = lax.dynamic_update_slice_in_dim(
                whole, piece.astype(dtype), first_at + core * half, 0
            )
            whole = lax.dynamic_update_slice_in_dim(
                whole, other.astype(dtype), first_at + (1 - core) * half, 0
            )
        return whole.reshape(rows, count, depth)

    last, _ = sum_grid(self_qkv_grad)
    source_grad = jnp.zeros((rows, slots, width), f32)
    for step, part in enumerate(source_parts):
        at = lax.rem(chip - step + chips, chips) * many
        source_grad = lax.dynamic_update_slice_in_dim(source_grad, part.astype(f32), at, 0)
    vector = late[depth : depth + lines].astype(f32).reshape(6, portion)
    late = late[:depth]

    def columns(array, first, size):
        return array[:, first : first + size].astype(f32)

    return (
        everywhere(results, bf16),
        everywhere(target_grads, f32),
        source_grad,
        columns(last, 0, width),
        columns(last, width, width),
        columns(last, 2 * width, width),
        columns(late, 0, width).T,
        columns(late, width, width),
        columns(middle, 2 * extra + width, width),
        columns(middle, 2 * extra + 2 * width, width),
        columns(middle, 2 * extra, width).T,
        columns(middle, extra, extra),
        columns(middle, 0, extra).T,
        vector[0],
        vector[1],
        vector[2],
        vector[3],
        vector[4],
        vector[5],
    )


def solution(mesh):
    return jax.shard_map(
        on_device,
        mesh=mesh,
        in_specs=(
            P("dp", "blk", None),
            P("dp", "blk", None),
            P("dp", "blk"),
            P("dp", "blk"),
            P(None, "tensor"),
            P(None, "tensor"),
            P(None, "tensor"),
            P("tensor", None),
            P(None, "tensor"),
            P(None, "tensor"),
            P(None, "tensor"),
            P("tensor", None),
            P(None, "tensor"),
            P("tensor", None),
            P(None, "tensor"),
            P("tensor", None),
            P(),
            P(),
            P(),
            P(),
            P(),
            P(),
            P("dp", "blk", None),
        ),
        out_specs=(
            P("dp", "blk", None),
            P("dp", "blk", None),
            P("dp", "blk", "tensor"),
            P(None, "tensor"),
            P(None, "tensor"),
            P(None, "tensor"),
            P("tensor", None),
            P(None, "tensor"),
            P(None, "tensor"),
            P(None, "tensor"),
            P("tensor", None),
            P(None, "tensor"),
            P("tensor", None),
            P("tensor"),
            P("tensor"),
            P("tensor"),
            P("tensor"),
            P("tensor"),
            P("tensor"),
        ),
        check_vma=False,
    )
```

```python
import functools

import jax
import jax.numpy as jnp
from jax import lax
from jax.experimental import pallas as pl
from jax.experimental.pallas import tpu as pltpu
from jax.sharding import PartitionSpec as P

HEAD_DIM = 64
HALO = 80
SOURCE_TILE = 512
FFN_TILE = 512
EXTRA = 16
VMEM_LIMIT = 40 * 2**20
VMEM_MOST = 56 * 2**20

epsilon = 1e-05
negative = -1e30
floor = -1e20
log2e = 1.4426950408889634
to_base2 = log2e * HEAD_DIM**-0.5
bf16 = jnp.bfloat16
f32 = jnp.float32


def forward_mul(left, right):
    return jnp.einsum("rti,ij->rtj", left, right, preferred_element_type=f32)


def backward_mul(left, right):
    return jnp.einsum("rtj,ij->rti", left, right, preferred_element_type=f32)


def weight_mul(left, right):
    return jnp.einsum("rti,rtj->ij", left, right, preferred_element_type=f32)


def norm_parts(values):
    centered = values - jnp.mean(values, axis=-1, keepdims=True)
    variance = jnp.mean(centered * centered, axis=-1, keepdims=True)
    scale = lax.rsqrt(variance + epsilon)
    return centered * scale, scale


def norm_back(unit, scale, gain, grad):
    inner = grad * gain
    first = jnp.mean(inner, axis=-1, keepdims=True)
    second = jnp.mean(inner * unit, axis=-1, keepdims=True)
    return (
        scale * (inner - first - unit * second),
        jnp.sum(grad * unit, axis=0),
        jnp.sum(grad, axis=0),
    )


def mul_nt(left, right):
    return lax.dot_general(left, right, (((1,), (1,)), ((), ())), preferred_element_type=f32)


def mul_nn(left, right):
    return lax.dot_general(left, right, (((1,), (0,)), ((), ())), preferred_element_type=f32)


def spread_heads(block, heads):
    if heads == 1:
        return block
    width = block.shape[1]
    lane = lax.broadcasted_iota(jnp.int32, (1, width), 1)
    copies = []
    for head in range(heads):
        inside = (lane >= head * HEAD_DIM) & (lane < (head + 1) * HEAD_DIM)
        copies.append(block * jnp.where(inside, 1.0, 0.0).astype(block.dtype))
    return jnp.concatenate(copies, axis=0)


def tile_lanes(block, heads):
    return jnp.concatenate([block] * heads, axis=1) if heads > 1 else block


def row_of(ref, heads):
    rows = [ref[0, head : head + 1, :] for head in range(heads)]
    return jnp.concatenate(rows, axis=1) if heads > 1 else rows[0]


def store_rows(ref, row, first, heads, count):
    for head in range(heads):
        ref[0, first + head : first + head + 1, :] = row[:, head * count : (head + 1) * count]


def rounded(row):
    return row.astype(bf16).astype(f32)


def pack_rows(ref, lines_ref, rows, width):
    line = 0
    for row in rows:
        for _ in range(3):
            term = rounded(row)
            row = row - term
            for at in range(0, term.shape[1], width):
                lines_ref[line : line + 1, :] = term[:, at : at + width]
                line += 1
    lines_ref[line:, :] = jnp.zeros((EXTRA - line, width), f32)
    ref[0, ref.shape[1] - EXTRA :, :] = lines_ref[...].astype(bf16)


def unpack_rows(ref, lines_ref, total, heads, count):
    width = ref.shape[2]
    lines = heads * count // width
    lines_ref[...] = ref[0, ref.shape[1] - EXTRA :, :].astype(f32)
    rows = []
    for index in range(total):
        pieces = []
        for at in range(lines):
            first = 3 * index * lines + at
            pieces.append(
                lines_ref[first : first + 1, :]
                + lines_ref[first + lines : first + lines + 1, :]
                + lines_ref[first + 2 * lines : first + 2 * lines + 1, :]
            )
        rows.append(jnp.concatenate(pieces, axis=1) if lines > 1 else pieces[0])
    return rows


def head_scale(row, heads, count):
    pieces = [
        jnp.broadcast_to(row[:, head * count : (head + 1) * count], (HEAD_DIM, count))
        for head in range(heads)
    ]
    return jnp.concatenate(pieces, axis=0) if heads > 1 else pieces[0]


def head_products(left, right, heads, count):
    pieces = [
        mul_nn(
            left[head * HEAD_DIM : (head + 1) * HEAD_DIM, :],
            right[:, head * count : (head + 1) * count],
        )
        for head in range(heads)
    ]
    return jnp.concatenate(pieces, axis=0) if heads > 1 else pieces[0]


def cross_forward_kernel(heads, blocks, tile, table_ref, *refs):
    queries = refs[:blocks]
    target_ids, source_ids, keys, values = refs[blocks : blocks + 4]
    mixed = refs[blocks + 4 : 2 * blocks + 4]
    turned, lines, total = refs[2 * blocks + 4 :]
    place = pl.program_id(0)
    count, width = queries[0].shape[1:]
    tiles = keys.shape[1] // tile
    for step in range(tiles):
        turned[step] = values[0, step * tile : (step + 1) * tile, :].T
    for block in range(blocks):
        spread = spread_heads(queries[block][0], heads)
        ids = target_ids[0, block : block + 1, :]
        total[...] = jnp.zeros_like(total)

        def visit(step, carry):
            best, weight = carry
            start = pl.multiple_of(step * tile, tile)
            scores = mul_nt(keys[0, pl.ds(start, tile), :], spread) * to_base2
            allowed = source_ids[0, pl.ds(start, tile), :] == ids
            scores = jnp.where(tile_lanes(allowed, heads), scores, negative)
            fresh = jnp.maximum(best, jnp.max(scores, axis=0, keepdims=True))
            anchor = jnp.maximum(fresh, floor)
            probs = jnp.exp2(scores - anchor)
            fade = jnp.exp2(best - anchor)
            weight = weight * fade + jnp.sum(probs, axis=0, keepdims=True)
            total[...] = total[...] * head_scale(fade, heads, count) + head_products(
                turned[step], probs.astype(bf16), heads, count
            )
            return fresh, weight

        best, weight = lax.fori_loop(
            table_ref[place, 2 * block],
            table_ref[place, 2 * block + 1],
            visit,
            (jnp.full((1, heads * count), negative, f32), jnp.zeros((1, heads * count), f32)),
        )
        some = weight > 0.0
        safe = jnp.where(some, weight, 1.0)
        scaled = total[...] * head_scale(1.0 / safe, heads, count)
        mixed[block][0, :count, :] = scaled.T.astype(bf16)
        sums = jnp.where(some, best + jnp.log2(safe), negative)
        pack_rows(mixed[block], lines.at[block], [sums], width)


def cross_merge_kernel(group, blocks, *refs):
    parts = refs[:blocks]
    weight, mixed, sums, product, lines = refs[blocks:]
    count, width = mixed.shape[1:]
    heads = group // HEAD_DIM
    for index in range(width // group):
        columns = slice(index * group, (index + 1) * group)
        rows = [
            unpack_rows(part.at[:, :, columns], lines.at[at], 1, heads, count)[0]
            for at, part in enumerate(parts)
        ]
        best = functools.reduce(jnp.maximum, rows)
        shares = [jnp.exp2(row - best) for row in rows]
        whole = functools.reduce(jnp.add, shares)
        store_rows(sums, best + jnp.log2(whole), index * heads, heads, count)
        inverse = 1.0 / whole
        total = None
        for part, each in zip(parts, shares):
            scale = head_scale(each * inverse, heads, count).T
            term = part[0, :count, columns].astype(f32) * scale
            total = term if total is None else total + term
        mixed[0, :, columns] = total.astype(bf16)
    product[0] = mul_nn(mixed[0], weight[...])


def cross_prepare_kernel(group, *refs):
    branch, weight, mixed, sums, message, lines = refs
    count, width = mixed.shape[1:]
    heads = group // HEAD_DIM
    grad = mul_nt(branch[0], weight[...]).astype(bf16)
    message[0, :count, :] = grad
    product = (grad.astype(f32) * mixed[0].astype(f32)).T
    for index in range(width // group):
        columns = slice(index * group, (index + 1) * group)
        delta, offset = [], []
        for head in range(index * heads, (index + 1) * heads):
            delta.append(
                jnp.sum(product[head * HEAD_DIM : (head + 1) * HEAD_DIM], axis=0, keepdims=True)
            )
            offset.append(sums[0, head : head + 1, :])
        if heads > 1:
            delta, offset = [jnp.concatenate(delta, axis=1)], [jnp.concatenate(offset, axis=1)]
        pack_rows(message.at[:, :, columns], lines, [offset[0], delta[0]], group)


def cross_backward_kernel(heads, blocks, tile, table_ref, *refs):
    queries = refs[:blocks]
    grads = refs[blocks : 2 * blocks]
    target_ids, source_ids, keys, values = refs[2 * blocks : 2 * blocks + 4]
    query_grads = refs[2 * blocks + 4 : 3 * blocks + 4]
    source_side, turned, lines, key_grad, value_grad, total = refs[3 * blocks + 4 :]
    place = pl.program_id(0)
    count, width = queries[0].shape[1:]
    tiles = keys.shape[1] // tile
    for step in range(tiles):
        turned[step] = keys[0, step * tile : (step + 1) * tile, :].T
    key_grad[...] = jnp.zeros_like(key_grad)
    value_grad[...] = jnp.zeros_like(value_grad)
    for block in range(blocks):
        spread = spread_heads(queries[block][0], heads)
        spread_grad = spread_heads(grads[block][0, :count, :], heads)
        offset, delta = unpack_rows(grads[block], lines.at[block], 2, heads, count)
        ids = target_ids[0, block : block + 1, :]
        total[...] = jnp.zeros_like(total)

        def visit(step, carry):
            start = pl.multiple_of(step * tile, tile)
            span = pl.ds(start, tile)
            scores = mul_nt(keys[0, span, :], spread) * to_base2
            allowed = source_ids[0, span, :] == ids
            probs = jnp.where(tile_lanes(allowed, heads), jnp.exp2(scores - offset), 0.0)
            dprobs = mul_nt(values[0, span, :], spread_grad)
            dscores = (probs * (dprobs - delta)).astype(bf16)
            key_grad[span, :] += mul_nn(dscores, spread)
            value_grad[span, :] += mul_nn(probs.astype(bf16), spread_grad)
            total[...] += head_products(turned[step], dscores, heads, count)
            return carry

        lax.fori_loop(table_ref[place, 2 * block], table_ref[place, 2 * block + 1], visit, 0)
        query_grads[block][0] = (total[...] * HEAD_DIM**-0.5).T.astype(bf16)
    source_side[0] = jnp.concatenate(
        [(key_grad[...] * HEAD_DIM**-0.5).astype(bf16), value_grad[...].astype(bf16)], axis=1
    )


def self_scores(heads, queries, keys, source_ids, ids):
    spread = spread_heads(queries, heads)
    scores = mul_nt(keys, spread) * to_base2
    count = queries.shape[0]
    slots = keys.shape[0]
    key_place = lax.broadcasted_iota(jnp.int32, (slots, count), 0) - (slots - count)
    query_place = lax.broadcasted_iota(jnp.int32, (slots, count), 1)
    allowed = (source_ids == ids) & (key_place <= query_place)
    return spread, scores, tile_lanes(allowed, heads)


def with_halo(halo, own):
    missing = own.shape[0] - halo.shape[0]
    return jnp.concatenate([jnp.zeros((missing, own.shape[1]), own.dtype), halo, own], axis=0)


def self_forward_kernel(heads, *refs):
    queries, keys, values, key_halo, value_halo, target_ids, source_ids, mixed, sums = refs
    count = queries.shape[1]
    every_key = with_halo(key_halo[0], keys[0])
    every_value = with_halo(value_halo[0], values[0])
    _, scores, allowed = self_scores(
        heads, queries[0], every_key, source_ids[0], target_ids[0, 0:1, :]
    )
    scores = jnp.where(allowed, scores, negative)
    best = jnp.max(scores, axis=0, keepdims=True)
    probs = jnp.exp2(scores - best)
    weight = jnp.sum(probs, axis=0, keepdims=True)
    total = head_products(every_value.T, probs.astype(bf16), heads, count)
    mixed[0] = (total * head_scale(1.0 / weight, heads, count)).T.astype(bf16)
    store_rows(sums, best + jnp.log2(weight), 0, heads, count)


def self_backward_kernel(heads, *refs):
    queries, keys, values, key_halo, value_halo, target_ids, source_ids, sums, grads = refs[:9]
    query_grad, key_own, value_own, side = refs[9:]
    count = queries.shape[1]
    every_key = with_halo(key_halo[0], keys[0])
    every_value = with_halo(value_halo[0], values[0])
    spread, scores, allowed = self_scores(
        heads, queries[0], every_key, source_ids[0], target_ids[0, 0:1, :]
    )
    spread_grad = spread_heads(grads[0], heads)
    probs = jnp.where(allowed, jnp.exp2(scores - row_of(sums, heads)), 0.0)
    dprobs = mul_nt(every_value, spread_grad)
    delta = jnp.sum(probs * dprobs, axis=0, keepdims=True)
    dscores = (probs * (dprobs - delta)).astype(bf16)
    key_grad = mul_nn(dscores, spread) * HEAD_DIM**-0.5
    value_grad = mul_nn(probs.astype(bf16), spread_grad)
    total = head_products(every_key.T, dscores, heads, count)
    query_grad[0] = (total * HEAD_DIM**-0.5).T.astype(bf16)
    slots = every_key.shape[0]
    first = slots - count - HALO
    key_own[0] = key_grad[slots - count :, :]
    value_own[0] = value_grad[slots - count :, :]
    side[0] = jnp.concatenate(
        [
            key_grad[first : slots - count, :].astype(bf16),
            value_grad[first : slots - count, :].astype(bf16),
        ],
        axis=1,
    )


def group_width(width, total):
    return width if width % 128 == 0 else total


def cross_call(backward, group, queries, grads, target_ids, source_ids, kv, table):
    blocks = len(queries)
    rows, count, width = queries[0].shape
    slots = kv.shape[1]
    tile = min(SOURCE_TILE, slots)
    heads = group // HEAD_DIM
    token = pl.BlockSpec((1, count, group), lambda i, g, t: (i, 0, g))
    packed = pl.BlockSpec((1, count + EXTRA, group), lambda i, g, t: (i, 0, g))
    in_specs = [token] * blocks
    operands = list(queries)
    if backward:
        in_specs += [packed] * blocks
        operands += list(grads)
    in_specs += [
        pl.BlockSpec((1, blocks, count), lambda i, g, t: (i, 0, 0)),
        pl.BlockSpec((1, slots, 1), lambda i, g, t: (i, 0, 0)),
        pl.BlockSpec((1, slots, group), lambda i, g, t: (i, 0, 2 * g)),
        pl.BlockSpec((1, slots, group), lambda i, g, t: (i, 0, 2 * g + 1)),
    ]
    operands += [target_ids, source_ids, kv, kv]
    scratch = [
        pltpu.VMEM((slots // tile, group, tile), bf16),
        pltpu.VMEM((blocks, EXTRA, group), f32),
    ]
    if backward:
        out_shape = [jax.ShapeDtypeStruct((rows, count, width), bf16)] * blocks
        out_shape += [jax.ShapeDtypeStruct((rows, slots, 2 * width), bf16)]
        out_specs = [token] * blocks + [
            pl.BlockSpec((1, slots, 2 * group), lambda i, g, t: (i, 0, g))
        ]
        scratch += [pltpu.VMEM((slots, group), f32), pltpu.VMEM((slots, group), f32)]
    else:
        out_shape = [jax.ShapeDtypeStruct((rows, count + EXTRA, width), bf16)] * blocks
        out_specs = [packed] * blocks
    scratch += [pltpu.VMEM((group, count), f32)]
    work = rows * slots * blocks * count * width // 2
    return pl.pallas_call(
        functools.partial(
            cross_backward_kernel if backward else cross_forward_kernel, heads, blocks, tile
        ),
        grid_spec=pltpu.PrefetchScalarGridSpec(
            num_scalar_prefetch=1,
            grid=(rows, width // group),
            in_specs=in_specs,
            out_specs=out_specs,
            scratch_shapes=scratch,
        ),
        out_shape=out_shape,
        compiler_params=pltpu.CompilerParams(vmem_limit_bytes=VMEM_MOST),
        cost_estimate=pl.CostEstimate(
            flops=work * (20 if backward else 8),
            bytes_accessed=rows * slots * width * (8 if backward else 4),
            transcendentals=0,
        ),
        name="cross_backward" if backward else "cross_forward",
    )(table, *operands)


def merge_call(group, parts, weight):
    rows, tall, width = parts[0].shape
    count = tall - EXTRA
    depth = weight.shape[1]
    heads = width // HEAD_DIM
    return pl.pallas_call(
        functools.partial(cross_merge_kernel, group, len(parts)),
        grid=(rows,),
        in_specs=[pl.BlockSpec((1, tall, width), lambda i: (i, 0, 0))] * len(parts)
        + [pl.BlockSpec(weight.shape, lambda i: (0, 0))],
        out_specs=[
            pl.BlockSpec((1, count, width), lambda i: (i, 0, 0)),
            pl.BlockSpec((1, heads, count), lambda i: (i, 0, 0)),
            pl.BlockSpec((1, count, depth), lambda i: (i, 0, 0)),
        ],
        out_shape=[
            jax.ShapeDtypeStruct((rows, count, width), bf16),
            jax.ShapeDtypeStruct((rows, heads, count), f32),
            jax.ShapeDtypeStruct((rows, count, depth), f32),
        ],
        scratch_shapes=[pltpu.VMEM((len(parts), EXTRA, group), f32)],
        compiler_params=pltpu.CompilerParams(vmem_limit_bytes=VMEM_LIMIT),
        cost_estimate=pl.CostEstimate(
            flops=2 * rows * count * width * depth,
            bytes_accessed=rows * tall * (width * 8 + depth * 4),
            transcendentals=0,
        ),
        name="cross_merge",
    )(*parts, weight)


def prepare_call(group, branch, weight, mixed, sums):
    rows, count, width = mixed.shape
    depth = branch.shape[2]
    heads = width // HEAD_DIM
    return pl.pallas_call(
        functools.partial(cross_prepare_kernel, group),
        grid=(rows,),
        in_specs=[
            pl.BlockSpec((1, count, depth), lambda i: (i, 0, 0)),
            pl.BlockSpec(weight.shape, lambda i: (0, 0)),
            pl.BlockSpec((1, count, width), lambda i: (i, 0, 0)),
            pl.BlockSpec((1, heads, count), lambda i: (i, 0, 0)),
        ],
        out_specs=pl.BlockSpec((1, count + EXTRA, width), lambda i: (i, 0, 0)),
        out_shape=jax.ShapeDtypeStruct((rows, count + EXTRA, width), bf16),
        scratch_shapes=[pltpu.VMEM((EXTRA, group), f32)],
        compiler_params=pltpu.CompilerParams(vmem_limit_bytes=VMEM_LIMIT),
        cost_estimate=pl.CostEstimate(
            flops=2 * rows * count * width * depth,
            bytes_accessed=rows * count * (width * 6 + depth * 2),
            transcendentals=0,
        ),
        name="cross_prepare",
    )(branch, weight, mixed, sums)


def mul_tn(left, right):
    return lax.dot_general(left, right, (((0,), (0,)), ((), ())), preferred_element_type=f32)


def project_kernel(row, tokens, weight, out):
    out[0] = mul_nn(tokens[0], weight[...]).astype(bf16)


def source_weight_kernel(row, tokens, grad, total):
    @pl.when((pl.program_id(0) == 0) & (pl.program_id(1) == 0))
    def _():
        total[...] = jnp.zeros_like(total)

    total[...] += mul_tn(tokens[0], grad[0])


def source_other_kernel(grad, weight, out):
    out[0] = mul_nt(grad[0], weight[...]).astype(bf16)


def source_own_kernel(grad, weight, across, own, peer):
    width = own.shape[2]
    total = mul_nt(grad[0], weight[...]) + across[0].astype(f32)
    own[0] = total[:, :width]
    peer[0] = total[:, width:].astype(bf16)


def source_call(kernel, row, rows, slots, operands, blocks, outs, name):
    tile = min(FFN_TILE, slots)
    prefetch = row is not None

    def spec(shape, kind):
        if kind == "all":
            return pl.BlockSpec(shape, lambda i, j, *r: (0, 0))
        if kind == "far":
            return pl.BlockSpec((1, tile, shape[2]), lambda i, j, r: (r[0] + i, j, 0))
        return pl.BlockSpec((1, tile, shape[2]), lambda i, j, *r: (i, j, 0))

    count = len(operands)
    return pl.pallas_call(
        kernel,
        grid_spec=pltpu.PrefetchScalarGridSpec(
            num_scalar_prefetch=1 if prefetch else 0,
            grid=(rows, slots // tile),
            in_specs=[spec(each.shape, kind) for each, kind in zip(operands, blocks)],
            out_specs=[spec(each.shape, kind) for each, kind in zip(outs, blocks[count:])],
        ),
        out_shape=outs,
        compiler_params=pltpu.CompilerParams(vmem_limit_bytes=VMEM_MOST),
        cost_estimate=pl.CostEstimate(flops=0, bytes_accessed=0, transcendentals=0),
        name=name,
    )(*([row] if prefetch else []), *operands)


def ffn_forward_kernel(tokens, weight_in, weight_out, down, up, total, slope, rect, down_slope):
    @pl.when(pl.program_id(0) == 0)
    def _():
        value = mul_nn(tokens[...], down[...])
        smooth = 1.0 / (1.0 + jnp.exp(-value))
        low = (value * smooth).astype(bf16)
        rect[...] = low
        down_slope[...] = smooth * (1.0 + value * (1.0 - smooth))
        total[...] = 4.0 * mul_nn(low, up[...])

    gate = mul_nn(tokens[...], weight_in[...])
    normal = 0.5 * (1.0 + lax.erf(gate * 0.5**0.5))
    slope[...] = (normal + gate * jnp.exp(-0.5 * gate * gate) * 0.3989422804014327).astype(bf16)
    total[...] += mul_nn((gate * normal).astype(bf16), weight_out[...])


def ffn_backward_kernel(grad, weight_in, weight_out, down, up, slope, down_slope, total, down_grad):
    @pl.when(pl.program_id(0) == 0)
    def _():
        low = (4.0 * mul_nt(grad[...], up[...]) * down_slope[...]).astype(bf16)
        down_grad[...] = low
        total[...] = mul_nt(low, down[...])

    gate_grad = (mul_nt(grad[...], weight_out[...]) * slope[...].astype(f32)).astype(bf16)
    total[...] += mul_nt(gate_grad, weight_in[...])


def ffn_call(backward, tokens, weight_in, weight_out, down, up, slopes=()):
    count, depth = tokens.shape
    hidden = weight_in.shape[1]
    extra = down.shape[1]
    tile = min(FFN_TILE, hidden)
    whole = lambda shape: pl.BlockSpec(shape, lambda j: (0, 0))
    across = pl.BlockSpec((count, tile), lambda j: (0, j))
    in_specs = [
        whole((count, depth)),
        pl.BlockSpec((depth, tile), lambda j: (0, j)),
        pl.BlockSpec((tile, depth), lambda j: (j, 0)),
        whole((depth, extra)),
        whole((extra, depth)),
    ]
    out_shape = [jax.ShapeDtypeStruct((count, depth), f32)]
    out_specs = [whole((count, depth))]
    if backward:
        in_specs += [across, whole((count, extra))]
        out_shape += [jax.ShapeDtypeStruct((count, extra), bf16)]
        out_specs += [whole((count, extra))]
    else:
        out_shape += [
            jax.ShapeDtypeStruct((count, hidden), bf16),
            jax.ShapeDtypeStruct((count, extra), bf16),
            jax.ShapeDtypeStruct((count, extra), f32),
        ]
        out_specs += [across, whole((count, extra)), whole((count, extra))]
    return pl.pallas_call(
        ffn_backward_kernel if backward else ffn_forward_kernel,
        grid=(hidden // tile,),
        in_specs=in_specs,
        out_specs=out_specs,
        out_shape=out_shape,
        compiler_params=pltpu.CompilerParams(vmem_limit_bytes=VMEM_LIMIT),
        cost_estimate=pl.CostEstimate(
            flops=4 * count * hidden * depth,
            bytes_accessed=4 * hidden * depth,
            transcendentals=0,
        ),
        name="ffn_backward" if backward else "ffn_forward",
    )(tokens, weight_in, weight_out, down, up, *slopes)


def self_call(backward, group, qkv, halo, extra, target_ids, source_ids):
    rows, count = qkv.shape[:2]
    width = qkv.shape[2] // 3
    groups = width // group
    heads = group // HEAD_DIM
    in_specs = [
        pl.BlockSpec((1, count, group), lambda i, g, at=at: (i, 0, 3 * g + at)) for at in range(3)
    ]
    in_specs += [
        pl.BlockSpec((1, HALO, group), lambda i, g, at=at: (i, 0, 2 * g + at)) for at in range(2)
    ]
    token = pl.BlockSpec((1, count, group), lambda i, g: (i, 0, g))
    stat = pl.BlockSpec((1, None, heads, count), lambda i, g: (i, g, 0, 0))
    in_specs += [
        pl.BlockSpec((1, 1, count), lambda i, g: (i, 0, 0)),
        pl.BlockSpec((1, 2 * count, 1), lambda i, g: (i, 0, 0)),
    ]
    operands = [qkv, qkv, qkv, halo, halo, target_ids, source_ids]
    token_shape = (rows, count, width)
    if backward:
        in_specs += [stat, token]
        operands += list(extra)
        out_shape = [
            jax.ShapeDtypeStruct(token_shape, bf16),
            jax.ShapeDtypeStruct(token_shape, f32),
            jax.ShapeDtypeStruct(token_shape, f32),
            jax.ShapeDtypeStruct((rows, HALO, 2 * width), bf16),
        ]
        out_specs = [
            token,
            token,
            token,
            pl.BlockSpec((1, HALO, 2 * group), lambda i, g: (i, 0, g)),
        ]
    else:
        out_shape = [
            jax.ShapeDtypeStruct(token_shape, bf16),
            jax.ShapeDtypeStruct((rows, groups, heads, count), f32),
        ]
        out_specs = [token, stat]
    work = rows * count * count * width
    return pl.pallas_call(
        functools.partial(self_backward_kernel if backward else self_forward_kernel, heads),
        grid=(rows, groups),
        in_specs=in_specs,
        out_specs=out_specs,
        out_shape=out_shape,
        compiler_params=pltpu.CompilerParams(vmem_limit_bytes=VMEM_LIMIT),
        cost_estimate=pl.CostEstimate(
            flops=work * (40 if backward else 16),
            bytes_accessed=rows * count * width * 12,
            transcendentals=0,
        ),
        name="self_backward" if backward else "self_forward",
    )(*operands)


def send_blk(array, distance, size):
    return lax.ppermute(array, "blk", [(i, (i + distance) % size) for i in range(size)])


def send_sibling(array, size):
    return lax.ppermute(array, "tensor", [(i, i ^ 1) for i in range(size)])


def send_outer(array, distance, size):
    return lax.ppermute(array, "tensor", [(i, (i + 2 * distance) % size) for i in range(size)])


def tie(token, *arrays):
    if token is None:
        return arrays
    return lax.optimization_barrier((token, *arrays))[1:]


def sum_grid(value, first=(), others_of=lambda first: ()):
    groups, blocks = lax.axis_size("dp"), lax.axis_size("blk")
    group, place = lax.axis_index("dp"), lax.axis_index("blk")
    depth, width = value.shape

    def send_dp(array, step):
        return lax.ppermute(array, "dp", [(i, (i + step) % groups) for i in range(groups)])

    def reduce_over(array, index, size, send):
        many = array.shape[0] // size
        mine = lax.dynamic_slice_in_dim(array, index * many, many, 0)
        for step in range(1, size):
            to = lax.rem(index + step, size)
            other = lax.dynamic_slice_in_dim(array, to * many, many, 0)
            mine = mine + send(other.astype(bf16), step).astype(f32)
        return mine

    def gather_over(array, index, size, send):
        many = array.shape[0]
        whole = jnp.zeros((many * size, width), array.dtype)
        whole = lax.dynamic_update_slice_in_dim(whole, array, index * many, 0)
        for step in range(1, size):
            source = lax.rem(index - step + size, size)
            whole = lax.dynamic_update_slice_in_dim(whole, send(array, step), source * many, 0)
        return whole

    def over_blk(array, step):
        return send_blk(array, step, blocks)

    total = reduce_over(value, group, groups, send_dp)
    total, first = lax.optimization_barrier((total, first))
    others = others_of(first)
    total = reduce_over(total, place, blocks, over_blk).astype(bf16)
    total = gather_over(total, place, blocks, over_blk)
    total, others = lax.optimization_barrier((total, others))
    return gather_over(total, group, groups, send_dp), others


def sum_small(value):
    groups, blocks = lax.axis_size("dp"), lax.axis_size("blk")
    total = value
    for step in range(1, groups):
        total = total + lax.ppermute(
            value, "dp", [(i, (i + step) % groups) for i in range(groups)]
        )
    value = total
    for step in range(1, blocks):
        total = total + send_blk(value, step, blocks)
    return total


def on_device(
    target,
    source,
    target_segments,
    source_segments,
    self_query,
    self_key,
    self_value,
    self_output,
    cross_query,
    cross_key,
    cross_value,
    cross_output,
    ffn_in,
    ffn_out,
    adapter_down,
    adapter_up,
    first_gain,
    first_shift,
    second_gain,
    second_shift,
    third_gain,
    third_shift,
    out_cotangent,
):
    rows, count, depth = target.shape
    slots = source.shape[1]
    width = self_query.shape[1]
    extra = adapter_up.shape[0]
    blocks = lax.axis_size("blk")
    lanes = lax.axis_size("tensor")
    place = lax.axis_index("blk")
    lane = lax.axis_index("tensor")
    core = lax.rem(lane, 2)
    chip = lane // 2
    chips = lanes // 2
    many = rows // chips
    half = many * count // 2
    tile = min(SOURCE_TILE, slots)
    wide = width * chips
    group = group_width(width, wide)
    groups = range(wide // group)

    def over_blk(array):
        return [array] + [send_blk(array, step, blocks) for step in range(1, blocks)]

    def back_blk(arrays):
        return [arrays[0]] + [send_blk(arrays[step], -step, blocks) for step in range(1, blocks)]

    def over_chips(array):
        return [array] + [send_outer(array, step, lanes) for step in range(1, chips)]

    def home_chips(arrays):
        total = arrays[0]
        for step in range(1, chips):
            total = total + send_outer(arrays[step].astype(bf16), -step, lanes).astype(f32)
        return total

    def packed_over_chips(*arrays):
        flat = jnp.concatenate([each.reshape(-1, depth) for each in arrays], axis=0)
        lists = [[each] for each in arrays]
        for step in range(1, chips):
            far = send_outer(flat, step, lanes)
            at = 0
            for each, gathered in zip(arrays, lists):
                size = each.size // depth
                gathered.append(far[at : at + size].reshape(each.shape))
                at += size
        return lists

    def chip_rows(array, step):
        at = lax.rem(chip + step, chips) * many
        return lax.dynamic_slice_in_dim(array, at, many, 0)

    def core_half(array):
        flat = array.reshape(many * count, array.shape[-1])
        return lax.dynamic_slice_in_dim(flat, core * half, half, 0)

    def share(mine):
        other = send_sibling(mine, lanes)
        first_one = core == 0
        both = [jnp.where(first_one, mine, other), jnp.where(first_one, other, mine)]
        return jnp.concatenate(both, axis=0).reshape(many, count, mine.shape[-1])

    def reduced(part):
        flat = part.reshape(many * count, part.shape[-1])
        other = lax.dynamic_slice_in_dim(flat, (1 - core) * half, half, 0).astype(bf16)
        return core_half(part) + send_sibling(other, lanes).astype(f32)

    def total_of(multiply, lefts, rights):
        return functools.reduce(jnp.add, [multiply(a, b) for a, b in zip(lefts, rights)])

    def by_group(*lists):
        joined = [jnp.concatenate(each, axis=-1) for each in lists]
        pieces = [
            each[..., at * group : (at + 1) * group] for at in groups for each in joined
        ]
        return jnp.concatenate(pieces, axis=-1)

    def ungroup(array, kinds):
        return [
            jnp.concatenate(
                [
                    array[..., (at * kinds + kind) * group : (at * kinds + kind + 1) * group]
                    for at in groups
                ],
                axis=-1,
            )
            for kind in range(kinds)
        ]

    def lane_columns(array):
        return [array[..., at * width : (at + 1) * width] for at in range(chips)]

    far_ids = over_blk(chip_rows(target_segments, 0))
    target_ids = jnp.stack(far_ids, axis=1)
    first_row = (chip * many).astype(jnp.int32).reshape(1)
    source_segments = chip_rows(source_segments, 0)
    tiles = source_segments.reshape(many, slots // tile, tile)
    table = jnp.stack(
        [
            jnp.sum(tiles[:, None, :, -1] < target_ids[:, :, :1], axis=-1, dtype=jnp.int32),
            jnp.sum(tiles[:, None, :, 0] <= target_ids[:, :, -1:], axis=-1, dtype=jnp.int32),
        ],
        axis=-1,
    ).reshape(many, 2 * blocks)
    source_ids = source_segments[:, :, None]
    halo_ids = jnp.where(place == 0, -1, far_ids[-1 + min(blocks, 2)][:, count - HALO :])
    self_ids = jnp.concatenate(
        [jnp.full((many, count - HALO), -1, jnp.int32), halo_ids, far_ids[0]], axis=1
    )[:, :, None]
    own_ids = target_ids[:, :1]

    qkv_weight = jnp.concatenate([self_query, self_key, self_value], axis=1)
    all_tokens = jnp.concatenate([chip_rows(target, step) for step in range(chips)], axis=0)
    tokens = all_tokens[:many]
    target_mine = core_half(tokens)
    flat_cotangent = out_cotangent.reshape(rows * count, depth)
    cotangent = lax.dynamic_slice_in_dim(
        flat_cotangent, chip * many * count + core * half, half, 0
    )
    self_outputs = over_chips(self_output)
    every = forward_mul(all_tokens, qkv_weight).astype(bf16)
    qkv = [every[:many]] + [
        send_outer(every[step * many : (step + 1) * many], step, lanes)
        for step in range(1, chips)
    ]
    arrived = qkv[-1]
    qkv = by_group(*[[each[..., at * width : (at + 1) * width] for each in qkv] for at in range(3)])
    halo = jnp.concatenate(
        [
            qkv[:, count - HALO :, (3 * at + 1) * group : (3 * at + 3) * group]
            for at in groups
        ],
        axis=2,
    )
    halo = send_blk(halo, 1, blocks)
    cross_queries = over_chips(tie(arrived, cross_query)[0])
    halo, cross_queries, self_outputs = lax.optimization_barrier(
        (halo, cross_queries, self_outputs)
    )

    self_low, self_sums = self_call(False, group, qkv, halo, (), own_ids, self_ids)
    self_outputs = jnp.concatenate(self_outputs, axis=0)
    first_in = target_mine.astype(f32) + reduced(forward_mul(self_low, self_outputs))
    first_unit, first_scale = norm_parts(first_in)
    first = first_unit * first_gain + first_shift
    first_low = share(first.astype(bf16))

    cross_queries = jnp.concatenate(cross_queries, axis=1)
    cross_q = forward_mul(first_low, cross_queries).astype(bf16)
    far_q = over_blk(cross_q)
    near_kv = tie(cross_q, jnp.concatenate([cross_key, cross_value], axis=1))[0]
    kv_weights = over_chips(near_kv)
    kv_weight = by_group(
        [each[:, :width] for each in kv_weights], [each[:, width:] for each in kv_weights]
    )
    (kv,) = source_call(
        project_kernel,
        first_row,
        many,
        slots,
        (source, kv_weight),
        ("far", "all", "near"),
        [jax.ShapeDtypeStruct((many, slots, 2 * wide), bf16)],
        "source_project",
    )
    near = tie(kv_weights[-1], cross_output, ffn_in, adapter_down)
    cross_outputs, ffn_ins = packed_over_chips(*near[:2])
    downs = over_chips(near[2])
    visited = cross_call(False, group, far_q, (), target_ids, source_ids, kv, table)
    back = back_blk(visited)
    ffn_outs, ups = packed_over_chips(*tie(visited[0], ffn_out, adapter_up))
    back, cross_outputs, ffn_ins, downs = lax.optimization_barrier(
        (back, cross_outputs, ffn_ins, downs)
    )
    cross_outputs = jnp.concatenate(cross_outputs, axis=0)
    down_weight = jnp.concatenate(downs, axis=1)
    ffn_in_weight = jnp.concatenate(ffn_ins, axis=1)
    ffn_out_weight = jnp.concatenate(ffn_outs, axis=0)
    up_weight = jnp.concatenate(ups, axis=0)
    cross_low, cross_sums, branch = merge_call(group, back, cross_outputs)
    second_in = first + reduced(branch)
    second_unit, second_scale = norm_parts(second_in)
    second = second_unit * second_gain + second_shift
    second_low = share(second.astype(bf16))

    ffn_weights = (ffn_in_weight, ffn_out_weight, down_weight, up_weight)
    branch, gate_slope, rectified, down_slope = ffn_call(
        False, second_low.reshape(many * count, depth), *ffn_weights
    )
    third_in = second + reduced(branch)
    third_unit, third_scale = norm_parts(third_in)
    result = (third_unit * third_gain + third_shift).astype(bf16)
    third_grad, third_gain_grad, third_shift_grad = norm_back(
        third_unit, third_scale, third_gain, cotangent.astype(f32)
    )
    branch_grad = share(third_grad.astype(bf16))

    branch, down_grad = ffn_call(
        True, branch_grad.reshape(many * count, depth), *ffn_weights, (gate_slope, down_slope)
    )
    second_grad = third_grad + reduced(branch)
    cross_grad, second_gain_grad, second_shift_grad = norm_back(
        second_unit, second_scale, second_gain, second_grad
    )
    cross_branch = share(cross_grad.astype(bf16))

    message = prepare_call(group, cross_branch, cross_outputs, cross_low, cross_sums)
    far_grads = over_blk(message)
    early = [
        jnp.concatenate(
            [
                4.0 * weight_mul(branch_grad, up),
                weight_mul(second_low, down),
                weight_mul(cross_branch, low),
            ],
            axis=1,
        )
        for up, down, low in zip(
            *[
                [
                    each.reshape(many, count, -1)[..., at * extra : (at + 1) * extra]
                    for at in range(chips)
                ]
                for each in (rectified, down_grad)
            ],
            lane_columns(cross_low),
        )
    ]
    early = home_chips(early)
    results = over_chips(tie(message, result)[0])
    far_grads, early, results = lax.optimization_barrier((far_grads, early, results))
    visited = cross_call(True, group, far_q, far_grads, target_ids, source_ids, kv, table)
    kv_grad = visited[blocks]
    back = back_blk(visited[:blocks])
    qkv_weights = over_chips(tie(kv_grad, qkv_weight)[0])
    (kv_grad_now,) = tie(back[min(1, blocks - 1)], kv_grad)

    def owner_rows(parity):
        owners = [lax.rem(chip + step, chips) * 2 + parity for step in range(chips)]
        rows_of = [
            lax.dynamic_slice_in_dim(kv_weight, owner * width, width, 0) for owner in owners
        ]
        return jnp.concatenate(rows_of, axis=0)

    (kv_weight_grad,) = source_call(
        source_weight_kernel,
        first_row,
        many,
        slots,
        (source, kv_grad_now),
        ("far", "near", "all"),
        [jax.ShapeDtypeStruct((depth, 2 * wide), f32)],
        "source_weight",
    )
    middle = [
        jnp.concatenate(each, axis=1)
        for each in zip(*[lane_columns(each) for each in ungroup(kv_weight_grad, 2)])
    ]
    (across,) = source_call(
        source_other_kernel,
        None,
        many,
        slots,
        (kv_grad_now, owner_rows(1 - core)),
        ("near", "all", "near"),
        [jax.ShapeDtypeStruct((many, slots, wide), bf16)],
        "source_other",
    )
    back, qkv_weights, middle, across = lax.optimization_barrier(
        (back, qkv_weights, middle, across)
    )
    cross_q_low = functools.reduce(jnp.add, [part.astype(f32) for part in back]).astype(bf16)
    first_grad = cross_grad + reduced(backward_mul(cross_q_low, cross_queries))
    self_grad, first_gain_grad, first_shift_grad = norm_back(
        first_unit, first_scale, first_gain, first_grad
    )
    middle = home_chips(list(tie(cross_q_low, *middle)))
    self_branch = share(self_grad.astype(bf16))

    mixed_grad = backward_mul(self_branch, self_outputs).astype(bf16)
    q_grad, key_own, value_own, side = self_call(
        True, group, qkv, halo, (self_sums, mixed_grad), own_ids, self_ids
    )
    side = lax.ppermute(side, "blk", [(i, i - 1) for i in range(1, blocks)])
    (middle,) = tie(q_grad, jnp.concatenate([early, middle], axis=1).astype(bf16))
    middle = lax.psum(middle, ("dp", "blk"))
    across = send_sibling(across, lanes)
    vector = jnp.stack(
        [
            first_gain_grad,
            first_shift_grad,
            second_gain_grad,
            second_shift_grad,
            third_gain_grad,
            third_shift_grad,
        ]
    )
    portion = depth // lanes
    lines = 6 * portion // (2 * width)
    below = 16 * lax.axis_size("dp") * blocks

    def vector_rows(step):
        owner = lax.rem(chip - step + chips, chips) * 2 + core
        piece = lax.dynamic_slice_in_dim(vector, owner * portion, portion, 1)
        return jnp.pad(piece.reshape(lines, 2 * width), ((0, below - lines), (0, 0)))

    vector, late_branch, late_low = tie(q_grad, vector, self_branch, first_low)
    vector = vector + send_sibling(vector, lanes)
    late = [
        jnp.concatenate([jnp.concatenate(each, axis=1), vector_rows(step)], axis=0)
        for step, each in enumerate(
            zip(
                lane_columns(weight_mul(late_branch, self_low)),
                lane_columns(weight_mul(late_low, cross_q_low)),
            )
        )
    ]
    late = home_chips(late)
    after = ((0, 0), (count - HALO, 0), (0, 0))
    key_side, value_side = [jnp.pad(each.astype(f32), after) for each in ungroup(side, 2)]
    key_grad = (key_own + key_side).astype(bf16)
    value_grad = (value_own + value_side).astype(bf16)
    qkv_grad = [
        jnp.concatenate(each, axis=2)
        for each in zip(lane_columns(q_grad), lane_columns(key_grad), lane_columns(value_grad))
    ]
    home = [qkv_grad[0]] + [
        send_outer(qkv_grad[step], -step, lanes) for step in range(1, chips)
    ]
    self_qkv_grad = weight_mul(all_tokens, jnp.concatenate(home, axis=0))
    source_own, source_peer = source_call(
        source_own_kernel,
        None,
        many,
        slots,
        (tie(home[-1], kv_grad)[0], owner_rows(core), across),
        ("near", "all", "near", "near", "near"),
        [
            jax.ShapeDtypeStruct((many, slots, width), f32),
            jax.ShapeDtypeStruct((many, slots, wide - width), bf16),
        ],
        "source_own",
    )

    def source_sends(first):
        own, peer = first
        far = [
            send_outer(peer[:, :, (step - 1) * width : step * width], step, lanes)
            for step in range(1, chips)
        ]
        return middle, [own] + far

    late, (middle, source_parts) = sum_grid(
        tie(self_qkv_grad, late)[0], (source_own, source_peer), source_sends
    )
    (self_grad, *qkv_grad) = tie(self_qkv_grad, self_grad, *qkv_grad)
    target_grad = self_grad + reduced(total_of(backward_mul, qkv_grad, qkv_weights))
    target_grads = over_chips(lax.optimization_barrier(target_grad.astype(bf16)))

    def everywhere(pieces, dtype):
        whole = jnp.zeros((rows * count, depth), dtype)
        for step, piece in enumerate(pieces):
            first_at = lax.rem(chip - step + chips, chips) * many * count
            other = send_sibling(piece, lanes)
            whole = lax.dynamic_update_slice_in_dim(
                whole, piece.astype(dtype), first_at + core * half, 0
            )
            whole = lax.dynamic_update_slice_in_dim(
                whole, other.astype(dtype), first_at + (1 - core) * half, 0
            )
        return whole.reshape(rows, count, depth)

    last, _ = sum_grid(self_qkv_grad)
    source_grad = jnp.zeros((rows, slots, width), f32)
    for step, part in enumerate(source_parts):
        at = lax.rem(chip - step + chips, chips) * many
        source_grad = lax.dynamic_update_slice_in_dim(source_grad, part.astype(f32), at, 0)
    vector = late[depth : depth + lines].astype(f32).reshape(6, portion)
    late = late[:depth]

    def columns(array, first, size):
        return array[:, first : first + size].astype(f32)

    return (
        everywhere(list(tie(q_grad, *results)), bf16),
        everywhere(target_grads, f32),
        source_grad,
        columns(last, 0, width),
        columns(last, width, width),
        columns(last, 2 * width, width),
        columns(late, 0, width).T,
        columns(late, width, width),
        columns(middle, 2 * extra + width, width),
        columns(middle, 2 * extra + 2 * width, width),
        columns(middle, 2 * extra, width).T,
        columns(middle, extra, extra),
        columns(middle, 0, extra).T,
        vector[0],
        vector[1],
        vector[2],
        vector[3],
        vector[4],
        vector[5],
    )


def solution(mesh):
    return jax.shard_map(
        on_device,
        mesh=mesh,
        in_specs=(
            P("dp", "blk", None),
            P("dp", "blk", None),
            P("dp", "blk"),
            P("dp", "blk"),
            P(None, "tensor"),
            P(None, "tensor"),
            P(None, "tensor"),
            P("tensor", None),
            P(None, "tensor"),
            P(None, "tensor"),
            P(None, "tensor"),
            P("tensor", None),
            P(None, "tensor"),
            P("tensor", None),
            P(None, "tensor"),
            P("tensor", None),
            P(),
            P(),
            P(),
            P(),
            P(),
            P(),
            P("dp", "blk", None),
        ),
        out_specs=(
            P("dp", "blk", None),
            P("dp", "blk", None),
            P("dp", "blk", "tensor"),
            P(None, "tensor"),
            P(None, "tensor"),
            P(None, "tensor"),
            P("tensor", None),
            P(None, "tensor"),
            P(None, "tensor"),
            P(None, "tensor"),
            P("tensor", None),
            P(None, "tensor"),
            P("tensor", None),
            P("tensor"),
            P("tensor"),
            P("tensor"),
            P("tensor"),
            P("tensor"),
            P("tensor"),
        ),
        check_vma=False,
    )
```
